128 devices in a mesh: space: 32 (over x, y, core), chan: 4 (over z).
Axes of the slice: x: 4, y: 4, z: 4, core: 2. Of those that a mesh axis runs over, the one named last changes fastest.
Arguments:
- grid_state: bfloat16 [262144, 512], P('space', 'chan'), may hold values from -6 to 6
- cotangent: bfloat16 [262144, 512], P('space', 'chan'), may hold values from -6 to 6
- encoder_weight: bfloat16 [512, 512], P(None, 'chan'), may hold values from -0.25 to 0.25
- processor_weight: bfloat16 [512, 512], P(None, 'chan'), may hold values from -0.25 to 0.25
- decoder_weight: bfloat16 [512, 512], P(None, 'chan'), may hold values from -0.25 to 0.25
- g2m_send: int32 [1024, 256], P('space'), may hold values from 0 to 8191
- g2m_edges: int32 [10240, 40], P('space'), may hold values from 0 to 8191, as said below
- m2g_send: int32 [1024, 40], P('space'), may hold values from 0 to 319
- m2g_edges: int32 [262144, 3], P('space'), may hold values from 0 to 1279
- m2m_edges: int32 [10240, 8], P('space'), may hold values from 0 to 10239, as said below
Outputs:
- prediction: bfloat16 [262144, 512], P('space', 'chan')
- grad_encoder: float32 [512, 512], P(None, 'chan')
- grad_processor: float32 [512, 512], P(None, 'chan')
- grad_decoder: float32 [512, 512], P(None, 'chan')
The draws below stay inside these ranges and needn't reach their ends.
Inputs may be any that keep to these rules, and one draw needn't show every extreme that they name: `g2m_send`: row s times the number of space devices plus p lists, slot by slot, the grid row local to device s that fills that slot for mesh owner p; a row may fill several slots. `g2m_edges`: each value is a slot of the rows received by the mesh node's own device; every such slot is named by some mesh node of that device. `m2g_send`: row s times the number of space devices plus p lists, slot by slot, the mesh row local to device s that fills that slot for grid owner p. `m2g_edges`: each value is a slot of the rows received by the grid node's own device. `m2m_edges`: each neighbour of mesh node m lies within 160 rows of m, counted cyclically over all 10240 rows.
All inputs are finite; a program needn't handle non-finite values.
Results may differ from the reference program's by a relative error of at most 0.0065.
Values may be sent and summed in bfloat16 or wider, within the bound.
A program may use at most 128 MiB of HBM per device.

```python
import jax
import jax.numpy as jnp

D = 512
G_DEV = 8192
M_DEV = 320
FAN_G2M = 40
FAN_M2M = 8
FAN_M2G = 3
REACH = 160
CAP = 256
CAP2 = 40
GRID = 262144
MESH = 10240
N_SPACE = 32


def draw_m2m_edges(key, part):
    key = jax.random.fold_in(key, 7)
    offsets = jax.random.randint(key, (MESH, FAN_M2M), -REACH, REACH + 1)
    nodes = jnp.arange(MESH, dtype=jnp.int32)[:, None]
    return ((nodes + offsets) % MESH).astype(jnp.int32)


def draw_g2m_edges(key, part):
    key = jax.random.fold_in(key, 11)
    device_keys = jax.random.split(key, N_SPACE)
    length = M_DEV * FAN_G2M

    def one_order(single):
        return jax.random.permutation(single, length)
    orders = jax.vmap(one_order)(device_keys)
    return (orders % (N_SPACE * CAP)).reshape(MESH, FAN_G2M).astype(jnp.int32)


def plant(array, rng, smallest, top_value):
    spot = [jax.random.randint(jax.random.fold_in(rng, axis), (), 0, length) for axis, length in enumerate(array.shape)]
    longest = array.shape.index(max(array.shape))
    beside = spot[:longest] + [(spot[longest] + 1) % array.shape[longest]] + spot[longest + 1:]
    return array.at[tuple(spot)].set(smallest).at[tuple(beside)].set(top_value)


def levels(own_key, extent, cuts, smallest, largest):
    def one(axis_at, parts):
        steps = jax.random.uniform(jax.random.fold_in(jax.random.fold_in(own_key, 6), axis_at), (parts,), jnp.float32, smallest / len(cuts), largest / len(cuts))
        return jnp.repeat(jnp.exp(steps), extent[axis_at] // parts).reshape((-1,) + (1,) * (len(extent) - axis_at - 1))

    factor_of = one(*cuts[0])
    for cut in cuts[1:]:
        factor_of = factor_of * one(*cut)
    return factor_of


def centred(key, dims, scale, limit, pieces=(), kind=jnp.bfloat16):
    values = jax.random.normal(key, dims, jnp.float32) * scale
    if len(pieces) > 0:
        values = levels(key, dims, pieces, -0.22, 0.18) * values
    return jnp.clip(values, min=-limit, max=limit).astype(kind)


def setup_inputs(seed: int = 0) -> dict:
    key_list = jax.random.split(jax.random.key(seed), 11)
    grid_state = centred(key_list[0], (GRID, D), 1.0, 6.0, ((0, 32), (1, 4)))
    cotangent = centred(key_list[1], (GRID, D), 1.0, 6.0, ((0, 32), (1, 4)))
    encoder_weight = centred(key_list[2], (D, D), D ** -0.5, 0.25, ((1, 4),))
    processor_weight = centred(key_list[3], (D, D), D ** -0.5, 0.25, ((1, 4),))
    decoder_weight = centred(key_list[4], (D, D), D ** -0.5, 0.25, ((1, 4),))
    g2m_send = plant(jax.random.randint(key_list[5], (N_SPACE * N_SPACE, CAP), 0, G_DEV), jax.random.fold_in(key_list[5], 1), 0, G_DEV - 1).astype(jnp.int32)
    g2m_edges = draw_g2m_edges(jax.random.fold_in(key_list[10], 71), 0)
    m2g_send = plant(jax.random.randint(key_list[7], (N_SPACE * N_SPACE, CAP2), 0, M_DEV), jax.random.fold_in(key_list[7], 1), 0, M_DEV - 1).astype(jnp.int32)
    m2g_edges = plant(jax.random.randint(key_list[8], (GRID, FAN_M2G), 0, N_SPACE * CAP2), jax.random.fold_in(key_list[8], 1), 0, (N_SPACE * CAP2) - 1).astype(jnp.int32)
    m2m_edges = draw_m2m_edges(jax.random.fold_in(key_list[10], 71), 0)
    return {"grid_state": grid_state, "cotangent": cotangent, "encoder_weight": encoder_weight, "processor_weight": processor_weight, "decoder_weight": decoder_weight, "g2m_send": g2m_send, "g2m_edges": g2m_edges, "m2g_send": m2g_send, "m2g_edges": m2g_edges, "m2m_edges": m2m_edges}


def silu_slope(values):
    sigmoid = jax.nn.sigmoid(values)
    return sigmoid * (1.0 + values * (1.0 - sigmoid))


def source_rows(send_table, edge_table, rows_dev, owner_rows):
    slot_count = send_table.shape[1]
    node_count = edge_table.shape[0]
    owners = (jnp.arange(node_count, dtype=jnp.int32) // owner_rows)[:, None]
    sources = edge_table // slot_count
    slots = edge_table % slot_count
    return sources * rows_dev + send_table[sources * N_SPACE + owners, slots]


def gather_rows(table, indices):
    summed = jnp.zeros((indices.shape[0], table.shape[1]), jnp.float32)
    for column in range(indices.shape[1]):
        summed = summed + table[indices[:, column]].astype(jnp.float32)
    return summed


def spread_rows(values, indices, segment_count):
    summed = jnp.zeros((segment_count, values.shape[1]), jnp.float32)
    for column in range(indices.shape[1]):
        summed = summed.at[indices[:, column]].add(values)
    return summed


def exact_dot(left, right):
    return jnp.dot(left.astype(jnp.float32), right.astype(jnp.float32), precision=jax.lax.Precision.HIGHEST, preferred_element_type=jnp.float32)


def reference(grid_state, cotangent, encoder_weight, processor_weight, decoder_weight, g2m_send, g2m_edges, m2g_send, m2g_edges, m2m_edges):
    g2m_sources = source_rows(g2m_send, g2m_edges, G_DEV, M_DEV)
    m2g_sources = source_rows(m2g_send, m2g_edges, M_DEV, G_DEV)
    encoded = jnp.dot(grid_state, encoder_weight, preferred_element_type=jnp.float32).astype(jnp.bfloat16)
    gathered_sum = gather_rows(encoded, g2m_sources) * FAN_G2M ** -0.5
    mesh_first = jax.nn.silu(gathered_sum).astype(jnp.bfloat16)
    projected = jnp.dot(mesh_first, processor_weight, preferred_element_type=jnp.float32).astype(jnp.bfloat16)
    neighbour_sum = gather_rows(projected, m2m_edges) * FAN_M2M ** -0.5
    mesh_second = (mesh_first.astype(jnp.float32) + jax.nn.silu(neighbour_sum)).astype(jnp.bfloat16)
    decoded = jnp.dot(mesh_second, decoder_weight, preferred_element_type=jnp.float32).astype(jnp.bfloat16)
    prediction = (grid_state.astype(jnp.float32) + gather_rows(decoded, m2g_sources) * FAN_M2G ** -0.5).astype(jnp.bfloat16)
    scaled_cotangent = cotangent.astype(jnp.float32) * FAN_M2G ** -0.5
    decoded_grad = spread_rows(scaled_cotangent, m2g_sources, MESH)
    grad_decoder = exact_dot(mesh_second.T, decoded_grad)
    second_grad = exact_dot(decoded_grad, decoder_weight.T)
    pre_grad = second_grad * silu_slope(neighbour_sum) * FAN_M2M ** -0.5
    projected_grad = spread_rows(pre_grad, m2m_edges, MESH)
    grad_processor = exact_dot(mesh_first.T, projected_grad)
    first_grad = second_grad + exact_dot(projected_grad, processor_weight.T)
    sum_grad = first_grad * silu_slope(gathered_sum) * FAN_G2M ** -0.5
    slots_dev = N_SPACE * CAP
    mesh_owner = (jnp.arange(MESH, dtype=jnp.int32) // M_DEV)[:, None]
    global_slot = mesh_owner * slots_dev + g2m_edges
    slot_grad = spread_rows(sum_grad, global_slot, N_SPACE * slots_dev)
    slot_ids = jnp.arange(N_SPACE * slots_dev, dtype=jnp.int32)
    slot_owner = slot_ids // slots_dev
    slot_value = slot_ids % slots_dev
    slot_source = slot_value // CAP
    slot_node = slot_source * G_DEV + g2m_send[slot_source * N_SPACE + slot_owner, slot_value % CAP]
    encoded_grad = jnp.zeros((GRID, slot_grad.shape[1]), jnp.float32).at[slot_node].add(slot_grad)
    grad_encoder = exact_dot(grid_state.T, encoded_grad)
    return prediction, grad_encoder, grad_processor, grad_decoder
```

```python
import functools

import jax
import jax.numpy as jnp
from jax import lax
from jax.experimental import pallas as pl
from jax.experimental.pallas import tpu as pltpu
from jax.sharding import PartitionSpec as P

REACH = 160
CHUNK = 512
MESH = pl.DeviceIdType.MESH
F32 = jnp.float32
BF16 = jnp.bfloat16


def dot(a, b):
    return jnp.dot(a, b, preferred_element_type=F32)


def dot_nt(a, b):
    return lax.dot_general(a, b, (((1,), (1,)), ((), ())), preferred_element_type=F32)


def dot_tn(a, b):
    return lax.dot_general(a, b, (((0,), (0,)), ((), ())), preferred_element_type=F32)


def slope(values):
    sigmoid = jax.nn.sigmoid(values)
    return sigmoid * (1.0 + values * (1.0 - sigmoid))


def row_iota(rows, lanes):
    return lax.broadcasted_iota(jnp.int32, (rows, lanes), 0).astype(F32).astype(BF16)


def ones_where(mask):
    return jnp.where(mask, jnp.ones((), BF16), jnp.zeros((), BF16))


def narrow(row, base):
    return (row - base).astype(F32).astype(BF16)


def kernel(
    sizes,
    grid_ref,
    cot_ref,
    we_ref,
    wp_ref,
    wd_ref,
    send_ref,
    key_ref,
    low_ref,
    mrow_ref,
    mcol_ref,
    edge_ref,
    rimt_ref,
    rim_ref,
    pred_ref,
    ge_ref,
    gp_ref,
    gd_ref,
    grid32,
    stage,
    sendbuf,
    recv,
    at,
    counts,
    slot_grad,
    back,
    sel,
    selt,
    rim,
    rimt,
    dgrad,
    second_part,
    second_recv,
    second,
    state_sum,
    state_full,
    gathered,
    first,
    first_full,
    ext,
    neighbour,
    mid_full,
    out_rows,
    slots,
    slots_t,
    rim_grad,
    halo_low,
    halo_high,
    proj_part,
    proj_recv,
    grads_a,
    grads_b,
    grecv_a,
    grecv_b,
    gout,
    ssem,
    rsem,
    gsem,
):
    ns, nc, fan, fan_m, fan_d = sizes
    me = lax.axis_index("space")
    my = lax.axis_index("chan")
    grid_rows, width = grid_ref.shape
    cap = send_ref.shape[1]
    mesh = state_sum.shape[0]
    cap2 = back.shape[1]
    heads = counts.shape[0]
    per = cap // 128
    reach = halo_low.shape[0]
    share = grads_b.shape[1]
    fan_scale = fan ** (-0.5)
    fan_m_scale = fan_m ** (-0.5)
    fan_d_scale = fan_d ** (-0.5)
    all_slots = ns * cap2
    nxt = lax.rem(me + 1, ns)
    prv = lax.rem(me + ns - 1, ns)

    def remote(src, dst, which, space, chan, rec=None):
        return pltpu.make_async_remote_copy(
            src_ref=src,
            dst_ref=dst,
            send_sem=ssem.at[which],
            recv_sem=rsem.at[which] if rec is None else rec,
            device_id=(space, chan),
            device_id_type=MESH,
        )

    def peers(body):
        def step(k, carry):
            body(lax.rem(me + k, ns))
            return carry

        lax.fori_loop(1, ns, step, 0)

    def chans(body):
        for k in range(1, nc):
            body(lax.rem(my + k, nc))

    def wait_chan(buf, which):
        part = buf.at[pl.ds(0, nc - 1)]
        remote(part, part, which, me, my).wait_recv()

    def wait_space(buf, which):
        part = buf.at[pl.ds(0, ns - 1)]
        remote(part, part, which, me, my).wait_recv()

    def sent(buf, count, which):
        part = buf.at[pl.ds(0, count)]
        remote(part, part, which, me, my).wait_send()

    barrier = pltpu.get_barrier_semaphore()

    def greet(peer):
        pl.semaphore_signal(barrier, inc=1, device_id=(peer, my), device_id_type=MESH)

    peers(greet)

    def greet_chan(c):
        pl.semaphore_signal(barrier, inc=1, device_id=(me, c), device_id_type=MESH)

    chans(greet_chan)

    def widen(i, carry):
        rows = pl.ds(pl.multiple_of(i * CHUNK, CHUNK), CHUNK)
        grid32[rows, :] = grid_ref[rows, :].astype(F32)
        return carry

    lax.fori_loop(0, grid_rows // CHUNK, widen, 0)
    pl.semaphore_wait(barrier, ns + nc - 2)

    def pick(peer):
        def some(i, carry):
            base = pl.multiple_of(i * 16, 16)
            for u in range(16):
                stage[pl.ds(base + u, 1), :] = grid32[pl.ds(send_ref[peer, base + u], 1), :]
            return carry

        lax.fori_loop(0, cap // 16, some, 0)

    def pick_and_send(peer):
        pick(peer)
        sendbuf[peer] = stage[...].astype(BF16)
        remote(sendbuf.at[peer], recv.at[me], 0, peer, my, gsem.at[me]).start()

    peers(pick_and_send)
    pick(me)
    recv[me] = stage[...].astype(BF16)

    iota = row_iota(128, 128)
    slot_grad[...] = jnp.zeros(slot_grad.shape, F32)

    def edge_step(i, carry):
        start = pl.multiple_of(i * CHUNK, CHUNK)
        rows = edge_ref[:, pl.ds(start, CHUNK)]
        for kb in range(all_slots // 128):
            cut = [narrow(rows[j : j + 1, :], kb * 128) for j in range(fan_d)]
            for lb in range(CHUNK // 128):
                total = None
                for j in range(fan_d):
                    one = ones_where(iota == cut[j][:, lb * 128 : (lb + 1) * 128])
                    total = one if total is None else total + one
                at[kb * 128 : (kb + 1) * 128, pl.ds(start + lb * 128, 128)] = total
        slot_grad[...] += dot(at[:, pl.ds(start, CHUNK)], cot_ref[pl.ds(start, CHUNK), :])
        return carry

    lax.fori_loop(0, grid_rows // CHUNK, edge_step, 0)
    slot_grad[...] = slot_grad[...] * fan_d_scale
    own_rows = pl.ds(pl.multiple_of(me * cap2, cap2), cap2)

    def send_back(peer):
        rows = pl.ds(pl.multiple_of(peer * cap2, cap2), cap2)
        remote(slot_grad.at[rows], back.at[me], 1, peer, my).start()

    peers(send_back)
    back[me] = slot_grad[own_rows, :]

    def count_step(g, carry):
        key = key_ref[pl.ds(g, 1), :]
        low = low_ref[pl.ds(g, 1), :]
        lanes = key.shape[1]
        big = row_iota(128, lanes)
        right = ones_where(big == narrow(low, 0))
        for kb in range(heads * 8 // 128):
            left = ones_where(big == narrow(key, kb * 128))
            counts[kb * 16 : (kb + 1) * 16, pl.ds(pl.multiple_of(g * 8, 8), 8), :] = dot_nt(
                left, right
            ).reshape(16, 8, 128)
        return carry

    lax.fori_loop(0, mesh // 8, count_step, 0)

    rows_iota = lax.broadcasted_iota(jnp.int32, (rimt.shape[0], mesh), 0)
    lane_iota = lax.broadcasted_iota(jnp.int32, (mesh, rim.shape[1]), 1)
    total_t = jnp.zeros(rimt.shape, F32)
    total = jnp.zeros(rim.shape, F32)
    for j in range(fan_m):
        total_t = total_t + jnp.where(rows_iota == rimt_ref[j : j + 1, :], 1.0, 0.0)
        total = total + jnp.where(lane_iota == rim_ref[:, j : j + 1], 1.0, 0.0)
    rimt[...] = total_t.astype(BF16)
    rim[...] = total.astype(BF16)
    selt[...] = jnp.where(
        lax.broadcasted_iota(jnp.int32, selt.shape, 0) == mrow_ref[...], 1.0, 0.0
    ).astype(BF16)
    sel[...] = jnp.where(
        lax.broadcasted_iota(jnp.int32, sel.shape, 1) == mcol_ref[...], 1.0, 0.0
    ).astype(BF16)

    wait_space(back, 1)
    dgrad[...] = dot(selt[...], back[...].reshape(all_slots, width).astype(BF16)).astype(BF16)
    for c in range(nc):
        second_part[c] = dot_nt(dgrad[...], wd_ref[c * width : (c + 1) * width, :]).astype(BF16)

    def send_second(c):
        remote(second_part.at[c], second_recv.at[my], 2, me, c).start()

    chans(send_second)
    second_recv[my] = second_part[my]

    def absorb(source):
        left = jnp.concatenate([counts[source * per + h] for h in range(per)], axis=1)
        return dot(left.astype(BF16), recv[source])

    state_sum[...] = absorb(me)

    def absorb_step(k, carry):
        source = lax.rem(me + ns - k, ns)
        remote(recv.at[source], recv.at[source], 0, me, my, gsem.at[source]).wait_recv()
        state_sum[...] += absorb(source)
        return carry

    lax.fori_loop(1, ns, absorb_step, 0)
    state_full[my] = state_sum[...].astype(BF16)

    def send_state(c):
        remote(state_full.at[my], state_full.at[my], 3, me, c).start()

    chans(send_state)

    wait_chan(second_recv, 2)
    total = second_recv[0].astype(F32)
    for c in range(1, nc):
        total = total + second_recv[c].astype(F32)
    second[...] = total

    wait_chan(state_full, 3)
    total = dot(state_full[0], we_ref[0:width, :])
    for c in range(1, nc):
        total = total + dot(state_full[c], we_ref[c * width : (c + 1) * width, :])
    total = total * fan_scale
    gathered[...] = total
    first_full[my] = (total * jax.nn.sigmoid(total)).astype(BF16)

    def send_first(c):
        remote(first_full.at[my], first_full.at[my], 4, me, c).start()

    chans(send_first)
    first[...] = first_full[my].astype(F32)
    wait_chan(first_full, 4)
    total = dot(first_full[0], wp_ref[0:width, :])
    for c in range(1, nc):
        total = total + dot(first_full[c], wp_ref[c * width : (c + 1) * width, :])
    ext[reach : reach + mesh, :] = total.astype(BF16)
    to_next = remote(
        ext.at[pl.ds(mesh, reach)], ext.at[pl.ds(0, reach)], 5, nxt, my
    )
    to_prev = remote(
        ext.at[pl.ds(reach, reach)], ext.at[pl.ds(reach + mesh, reach)], 6, prv, my
    )
    to_next.start()
    to_prev.start()
    to_next.wait()
    to_prev.wait()
    total = dot(rim[...], ext[...]) * fan_m_scale
    neighbour[...] = total
    mid_full[my] = (first[...] + total * jax.nn.sigmoid(total)).astype(BF16)

    def send_mid(c):
        remote(mid_full.at[my], mid_full.at[my], 7, me, c).start()

    chans(send_mid)
    pre = (second[...] * slope(neighbour[...]) * fan_m_scale).astype(BF16)
    rim_grad[...] = dot(rimt[...], pre)
    down = remote(rim_grad.at[pl.ds(0, reach)], halo_high, 8, prv, my)
    up = remote(rim_grad.at[pl.ds(reach + mesh, reach)], halo_low, 9, nxt, my)
    down.start()
    up.start()

    wait_chan(mid_full, 7)
    total = dot(mid_full[0], wd_ref[0:width, :])
    for c in range(1, nc):
        total = total + dot(mid_full[c], wd_ref[c * width : (c + 1) * width, :])
    out_rows[...] = dot(sel[...], total.astype(BF16)).reshape(out_rows.shape)

    def send_rows(peer):
        remote(out_rows.at[peer], slots.at[me], 10, peer, my).start()

    peers(send_rows)
    slots[me] = out_rows[me]

    down.wait()
    up.wait()
    rim_grad[reach : 2 * reach, :] += halo_low[...]
    rim_grad[mesh : mesh + reach, :] += halo_high[...]
    projected = rim_grad[reach : reach + mesh, :].astype(BF16)
    for c in range(nc):
        proj_part[c] = dot_nt(projected, wp_ref[c * width : (c + 1) * width, :]).astype(BF16)

    def send_proj(c):
        remote(proj_part.at[c], proj_recv.at[my], 11, me, c).start()

    chans(send_proj)
    proj_recv[my] = proj_part[my]
    blocks = width // share
    for c in range(nc):
        cut = slice(c * blocks, (c + 1) * blocks)
        grads_a[cut, 0:share, :] = (
            dot_tn(mid_full[c], dgrad[...]).astype(BF16).reshape(blocks, share, width)
        )
        grads_a[cut, share : 2 * share, :] = (
            dot_tn(first_full[c], projected).astype(BF16).reshape(blocks, share, width)
        )

    def send_a(peer):
        remote(grads_a.at[peer], grecv_a.at[me], 12, peer, my).start()

    peers(send_a)
    grecv_a[me] = grads_a[me]

    wait_chan(proj_recv, 11)
    total = second[...]
    for c in range(nc):
        total = total + proj_recv[c].astype(F32)
    sum_grad = (total * slope(gathered[...]) * fan_scale).astype(BF16)
    for c in range(nc):
        cut = slice(c * blocks, (c + 1) * blocks)
        grads_b[cut] = (
            dot_tn(state_full[c], sum_grad).astype(BF16).reshape(blocks, share, width)
        )

    def send_b(peer):
        remote(grads_b.at[peer], grecv_b.at[me], 13, peer, my).start()

    peers(send_b)
    grecv_b[me] = grads_b[me]

    wait_space(slots, 10)
    slots_t[...] = slots[...].reshape(all_slots, width).T.astype(BF16)

    def predict(i, carry):
        start = pl.multiple_of(i * CHUNK, CHUNK)
        moved = dot(slots_t[...], at[:, pl.ds(start, CHUNK)]) * fan_d_scale
        rows = pl.ds(start, CHUNK)
        pred_ref[rows, :] = (grid_ref[rows, :].astype(F32) + moved.T).astype(BF16)
        return carry

    steps = grid_rows // CHUNK
    lax.fori_loop(0, steps // 2, predict, 0)

    wait_space(grecv_a, 12)
    wait_space(grecv_b, 13)
    total_a = grecv_a[0].astype(F32)
    total_b = grecv_b[0].astype(F32)
    for s in range(1, ns):
        total_a = total_a + grecv_a[s].astype(F32)
        total_b = total_b + grecv_b[s].astype(F32)
    gout[me, 0 : 2 * share, :] = total_a.astype(BF16)
    gout[me, 2 * share : 3 * share, :] = total_b.astype(BF16)

    def send_out(peer):
        remote(gout.at[me], gout.at[me], 14, peer, my).start()

    peers(send_out)
    lax.fori_loop(steps // 2, steps, predict, 0)
    wait_space(gout, 14)
    whole = gout[...].astype(F32)
    gd_ref[...] = whole[:, 0:share, :].reshape(gd_ref.shape)
    gp_ref[...] = whole[:, share : 2 * share, :].reshape(gp_ref.shape)
    ge_ref[...] = whole[:, 2 * share : 3 * share, :].reshape(ge_ref.shape)

    sent(sendbuf, ns - 1, 0)
    sent(back, ns - 1, 1)
    sent(second_part, nc - 1, 2)
    sent(state_full, nc - 1, 3)
    sent(first_full, nc - 1, 4)
    sent(mid_full, nc - 1, 7)
    sent(out_rows, ns - 1, 10)
    sent(proj_part, nc - 1, 11)
    sent(grads_a, ns - 1, 12)
    sent(grads_b, ns - 1, 13)
    sent(gout, ns - 1, 14)


def local(
    grid_state,
    cotangent,
    encoder_weight,
    processor_weight,
    decoder_weight,
    g2m_send,
    g2m_edges,
    m2g_send,
    m2g_edges,
    m2m_edges,
):
    ns = lax.axis_size("space")
    nc = lax.axis_size("chan")
    me = lax.axis_index("space")
    grid_rows, width = grid_state.shape
    mesh, fan = g2m_edges.shape
    fan_m = m2m_edges.shape[1]
    fan_d = m2g_edges.shape[1]
    cap = g2m_send.shape[1]
    cap2 = m2g_send.shape[1]
    reach = min(REACH, mesh // 2)
    full = encoder_weight.shape[0]
    share = full // ns
    heads = ns * cap // 128

    node = lax.broadcasted_iota(jnp.int32, g2m_edges.shape, 0)
    key = ((g2m_edges // 128) * 8 + node % 8).reshape(mesh // 8, 8 * fan)
    low = (g2m_edges % 128).reshape(mesh // 8, 8 * fan)
    rows = lax.broadcasted_iota(jnp.int32, (fan_m, mesh), 1)
    rim_t = (m2m_edges.T - me * mesh - rows + reach) % (ns * mesh) + rows
    rim = rim_t.T
    flat = m2g_send.reshape(1, ns * cap2)

    vmem = pl.BlockSpec(memory_space=pltpu.VMEM)
    smem = pl.BlockSpec(memory_space=pltpu.SMEM)
    weight = jax.ShapeDtypeStruct((full, width), F32)
    return tuple(
        pl.pallas_call(
            functools.partial(kernel, (ns, nc, fan, fan_m, fan_d)),
            out_shape=(
                jax.ShapeDtypeStruct(grid_state.shape, BF16),
                weight,
                weight,
                weight,
            ),
            in_specs=[vmem] * 5 + [smem] + [vmem] * 7,
            out_specs=(vmem,) * 4,
            scratch_shapes=[
                pltpu.VMEM((grid_rows, width), F32),
                pltpu.VMEM((cap, width), F32),
                pltpu.VMEM((ns, cap, width), BF16),
                pltpu.VMEM((ns, cap, width), BF16),
                pltpu.VMEM((ns * cap2, grid_rows), BF16),
                pltpu.VMEM((heads, mesh, 128), F32),
                pltpu.VMEM((ns * cap2, width), F32),
                pltpu.VMEM((ns, cap2, width), F32),
                pltpu.VMEM((ns * cap2, mesh), BF16),
                pltpu.VMEM((mesh, ns * cap2), BF16),
                pltpu.VMEM((mesh, mesh + 2 * reach), BF16),
                pltpu.VMEM((mesh + 2 * reach, mesh), BF16),
                pltpu.VMEM((mesh, width), BF16),
                pltpu.VMEM((nc, mesh, width), BF16),
                pltpu.VMEM((nc, mesh, width), BF16),
                pltpu.VMEM((mesh, width), F32),
                pltpu.VMEM((mesh, width), F32),
                pltpu.VMEM((nc, mesh, width), BF16),
                pltpu.VMEM((mesh, width), F32),
                pltpu.VMEM((mesh, width), F32),
                pltpu.VMEM((nc, mesh, width), BF16),
                pltpu.VMEM((mesh + 2 * reach, width), BF16),
                pltpu.VMEM((mesh, width), F32),
                pltpu.VMEM((nc, mesh, width), BF16),
                pltpu.VMEM((ns, cap2, width), F32),
                pltpu.VMEM((ns, cap2, width), F32),
                pltpu.VMEM((width, ns * cap2), BF16),
                pltpu.VMEM((mesh + 2 * reach, width), F32),
                pltpu.VMEM((reach, width), F32),
                pltpu.VMEM((reach, width), F32),
                pltpu.VMEM((nc, mesh, width), BF16),
                pltpu.VMEM((nc, mesh, width), BF16),
                pltpu.VMEM((ns, 2 * share, width), BF16),
                pltpu.VMEM((ns, share, width), BF16),
                pltpu.VMEM((ns, 2 * share, width), BF16),
                pltpu.VMEM((ns, share, width), BF16),
                pltpu.VMEM((ns, 3 * share, width), BF16),
                pltpu.SemaphoreType.DMA((15,)),
                pltpu.SemaphoreType.DMA((15,)),
                pltpu.SemaphoreType.DMA((ns,)),
            ],
            compiler_params=pltpu.CompilerParams(
                collective_id=0,
                has_side_effects=True,
                vmem_limit_bytes=62 * 1024 * 1024,
            ),
            cost_estimate=pl.CostEstimate(
                flops=12_000_000_000, bytes_accessed=10_000_000, transcendentals=0
            ),
            name="encode_process_decode",
        )(
            grid_state,
            cotangent,
            encoder_weight,
            processor_weight,
            decoder_weight,
            g2m_send,
            key,
            low,
            flat,
            flat.reshape(ns * cap2, 1),
            m2g_edges.T,
            rim_t,
            rim,
        )
    )


def solution(mesh):
    placed = (P("space", "chan"),) * 2 + (P(None, "chan"),) * 3 + (P("space", None),) * 5
    return jax.shard_map(
        local,
        mesh=mesh,
        in_specs=placed,
        out_specs=(P("space", "chan"),) + (P(None, "chan"),) * 3,
        check_vma=False,
    )
```

```python
import functools

import jax
import jax.numpy as jnp
from jax import lax
from jax.experimental import pallas as pl
from jax.experimental.pallas import tpu as pltpu
from jax.sharding import PartitionSpec as P

REACH = 160
CHUNK = 1024
MESH = pl.DeviceIdType.MESH
F32 = jnp.float32
BF16 = jnp.bfloat16


def dot(a, b):
    return jnp.dot(a, b, preferred_element_type=F32)


def dot_nt(a, b):
    return lax.dot_general(a, b, (((1,), (1,)), ((), ())), preferred_element_type=F32)


def dot_tn(a, b):
    return lax.dot_general(a, b, (((0,), (0,)), ((), ())), preferred_element_type=F32)


def slope(values):
    sigmoid = jax.nn.sigmoid(values)
    return sigmoid * (1.0 + values * (1.0 - sigmoid))


def row_iota(rows, lanes):
    return lax.broadcasted_iota(jnp.int32, (rows, lanes), 0).astype(F32).astype(BF16)


def ones_where(mask):
    return jnp.where(mask, jnp.ones((), BF16), jnp.zeros((), BF16))


def narrow(row, base):
    return (row - base).astype(F32).astype(BF16)


def kernel(
    sizes,
    grid_ref,
    cot_ref,
    we_ref,
    wp_ref,
    wd_ref,
    send_ref,
    source_ref,
    mesh_send_ref,
    edge_ref,
    near_ref,
    pred_ref,
    ge_ref,
    gp_ref,
    gd_ref,
    grid32,
    stage,
    sendbuf,
    recv,
    at_even,
    at_odd,
    key,
    low,
    counts,
    slot_grad,
    back,
    sel32,
    sel,
    selt,
    rim,
    rimt,
    dgrad,
    second_part,
    second_recv,
    second,
    state_sum,
    state_full,
    gathered,
    first,
    first_full,
    ext,
    neighbour,
    mid_full,
    out_rows,
    slots,
    slots_t,
    rim_grad,
    halo_low,
    halo_high,
    proj_part,
    proj_recv,
    grads_a,
    grads_b,
    grecv_a,
    grecv_b,
    gout,
    ssem,
    rsem,
    gsem,
):
    ns, nc, fan, fan_m, fan_d = sizes
    me = lax.axis_index("space")
    my = lax.axis_index("chan")
    grid_rows, width = grid_ref.shape
    cap = send_ref.shape[1]
    mesh = state_sum.shape[0]
    cap2 = back.shape[1]
    heads = counts.shape[0]
    per = cap // 128
    reach = halo_low.shape[0]
    share = grads_b.shape[1]
    fan_scale = fan ** (-0.5)
    fan_m_scale = fan_m ** (-0.5)
    fan_d_scale = fan_d ** (-0.5)
    all_slots = ns * cap2
    nxt = lax.rem(me + 1, ns)
    prv = lax.rem(me + ns - 1, ns)

    def remote(src, dst, which, space, chan, rec=None):
        return pltpu.make_async_remote_copy(
            src_ref=src,
            dst_ref=dst,
            send_sem=ssem.at[which],
            recv_sem=rsem.at[which] if rec is None else rec,
            device_id=(space, chan),
            device_id_type=MESH,
        )

    def peers(body):
        def step(k, carry):
            body(lax.rem(me + k, ns))
            return carry

        lax.fori_loop(1, ns, step, 0)

    def chans(body):
        for k in range(1, nc):
            body(lax.rem(my + k, nc))

    def wait_chan(buf, which):
        part = buf.at[pl.ds(0, nc - 1)]
        remote(part, part, which, me, my).wait_recv()

    def wait_space(buf, which):
        part = buf.at[pl.ds(0, ns - 1)]
        remote(part, part, which, me, my).wait_recv()

    def sent(buf, count, which):
        part = buf.at[pl.ds(0, count)]
        remote(part, part, which, me, my).wait_send()

    barrier = pltpu.get_barrier_semaphore()

    def greet(peer):
        pl.semaphore_signal(barrier, inc=1, device_id=(peer, my), device_id_type=MESH)

    peers(greet)

    def greet_chan(c):
        pl.semaphore_signal(barrier, inc=1, device_id=(me, c), device_id_type=MESH)

    chans(greet_chan)

    def widen(i, carry):
        rows = pl.ds(pl.multiple_of(i * CHUNK, CHUNK), CHUNK)
        grid32[rows, :] = grid_ref[rows, :].astype(F32)
        return carry

    lax.fori_loop(0, grid_rows // CHUNK, widen, 0)
    pl.semaphore_wait(barrier, ns + nc - 2)

    def pick(peer):
        def some(i, carry):
            base = pl.multiple_of(i * 32, 32)
            rows = [grid32[pl.ds(send_ref[peer, base + u], 1), :] for u in range(32)]
            for u in range(32):
                stage[pl.ds(base + u, 1), :] = rows[u]
            return carry

        lax.fori_loop(0, cap // 32, some, 0)

    def pick_and_send(peer):
        pick(peer)
        sendbuf[peer] = stage[...].astype(BF16)
        remote(sendbuf.at[peer], recv.at[me], 0, peer, my, gsem.at[me]).start()

    peers(pick_and_send)
    pick(me)
    recv[me] = stage[...].astype(BF16)

    iota = row_iota(128, 128)
    slot_grad[...] = jnp.zeros(slot_grad.shape, F32)

    steps = grid_rows // CHUNK
    half = all_slots // 2

    def build(buf, at, step, lo, hi):
        start = pl.multiple_of(step * CHUNK, CHUNK)
        rows = edge_ref[:, pl.ds(start, CHUNK)]
        for kb in range(lo // 128, hi // 128):
            cut = [narrow(rows[j : j + 1, :], kb * 128) for j in range(fan_d)]
            for lb in range(CHUNK // 128):
                total = None
                for j in range(fan_d):
                    one = ones_where(iota == cut[j][:, lb * 128 : (lb + 1) * 128])
                    total = one if total is None else total + one
                buf[at, kb * 128 : (kb + 1) * 128, lb * 128 : (lb + 1) * 128] = total

    def spread(buf, at, step, lo, hi):
        rows = pl.ds(pl.multiple_of(step * CHUNK, CHUNK), CHUNK)
        slot_grad[lo:hi, :] += dot(buf[at, lo:hi, :], cot_ref[rows, :])

    cuts = [(0, half), (half, all_slots)] if half % 128 == 0 else [(0, all_slots)]
    build(at_even, 0, 0, 0, all_slots)

    def edge_step(t, carry):
        for lo, hi in cuts:
            spread(at_even, t, 2 * t, lo, hi)
            build(at_odd, t, 2 * t + 1, lo, hi)
        for lo, hi in cuts:
            spread(at_odd, t, 2 * t + 1, lo, hi)
            build(at_even, t + 1, 2 * t + 2, lo, hi)
        return carry

    last = steps // 2 - 1
    lax.fori_loop(0, last, edge_step, 0)
    for lo, hi in cuts:
        spread(at_even, last, 2 * last, lo, hi)
        build(at_odd, last, 2 * last + 1, lo, hi)
    spread(at_odd, last, 2 * last + 1, 0, all_slots)
    slot_grad[...] = slot_grad[...] * fan_d_scale
    own_rows = pl.ds(pl.multiple_of(me * cap2, cap2), cap2)

    def send_back(peer):
        rows = pl.ds(pl.multiple_of(peer * cap2, cap2), cap2)
        remote(slot_grad.at[rows], back.at[me], 1, peer, my).start()

    peers(send_back)
    back[me] = slot_grad[own_rows, :]

    octets = mesh // 8
    parts = [source_ref[pl.ds(u, octets, stride=8), :] for u in range(8)]
    key[...] = jnp.concatenate([(part // 128) * 8 + u for u, part in enumerate(parts)], axis=1)
    low[...] = jnp.concatenate([part % 128 for part in parts], axis=1)
    big = row_iota(128, key.shape[1])

    def count_step(g, carry):
        found = []
        for u in range(2):
            top = key[pl.ds(2 * g + u, 1), :]
            right = ones_where(big == narrow(low[pl.ds(2 * g + u, 1), :], 0))
            found.append(
                [
                    dot_nt(ones_where(big == narrow(top, kb * 128)), right).reshape(16, 8, 128)
                    for kb in range(heads * 8 // 128)
                ]
            )
        rows = pl.ds(pl.multiple_of(g * 16, 16), 16)
        for kb in range(heads * 8 // 128):
            pair = jnp.concatenate([found[0][kb], found[1][kb]], axis=1)
            counts[kb * 16 : (kb + 1) * 16, rows, :] = pair.astype(BF16)
        return carry

    lax.fori_loop(0, mesh // 16, count_step, 0, unroll=2)

    node = lax.broadcasted_iota(jnp.int32, near_ref.shape, 1)
    span = ns * mesh
    offset = near_ref[...] - me * mesh - node + reach
    offset = jnp.where(offset < 0, offset + span, offset)
    offset = jnp.where(offset >= span, offset - span, offset) + node
    rows_iota = lax.broadcasted_iota(jnp.int32, rimt.shape, 0)
    total = jnp.zeros(rimt.shape, F32)
    for j in range(fan_m):
        total = total + jnp.where(rows_iota == offset[j : j + 1, :], 1.0, 0.0)
    rimt[...] = total.astype(BF16)
    rim[...] = total.T.astype(BF16)
    lane_iota = lax.broadcasted_iota(jnp.int32, (cap2, mesh), 1)
    for p in range(ns):
        column = mesh_send_ref[:, p : p + 1]
        sel32[p * cap2 : (p + 1) * cap2, :] = jnp.where(lane_iota == column, 1.0, 0.0)
    sel[...] = sel32[...].astype(BF16)
    selt[...] = sel32[...].T.astype(BF16)

    wait_space(back, 1)
    dgrad[...] = dot(selt[...], back[...].reshape(all_slots, width).astype(BF16)).astype(BF16)
    for c in range(nc):
        second_part[c] = dot_nt(dgrad[...], wd_ref[c * width : (c + 1) * width, :]).astype(BF16)

    def send_second(c):
        remote(second_part.at[c], second_recv.at[my], 2, me, c).start()

    chans(send_second)
    second_recv[my] = second_part[my]

    def absorb(source):
        left = jnp.concatenate([counts[source * per + h] for h in range(per)], axis=1)
        return dot(left, recv[source])

    state_sum[...] = absorb(me)

    def absorb_step(k, carry):
        source = lax.rem(me + ns - k, ns)
        remote(recv.at[source], recv.at[source], 0, me, my, gsem.at[source]).wait_recv()
        state_sum[...] += absorb(source)
        return carry

    lax.fori_loop(1, ns, absorb_step, 0)
    state_full[my] = state_sum[...].astype(BF16)

    def send_state(c):
        remote(state_full.at[my], state_full.at[my], 3, me, c).start()

    chans(send_state)

    wait_chan(second_recv, 2)
    total = second_recv[0].astype(F32)
    for c in range(1, nc):
        total = total + second_recv[c].astype(F32)
    second[...] = total

    wait_chan(state_full, 3)
    total = dot(state_full[0], we_ref[0:width, :])
    for c in range(1, nc):
        total = total + dot(state_full[c], we_ref[c * width : (c + 1) * width, :])
    total = total * fan_scale
    gathered[...] = total
    first_full[my] = (total * jax.nn.sigmoid(total)).astype(BF16)

    def send_first(c):
        remote(first_full.at[my], first_full.at[my], 4, me, c).start()

    chans(send_first)
    first[...] = first_full[my].astype(F32)
    wait_chan(first_full, 4)
    total = dot(first_full[0], wp_ref[0:width, :])
    for c in range(1, nc):
        total = total + dot(first_full[c], wp_ref[c * width : (c + 1) * width, :])
    ext[reach : reach + mesh, :] = total.astype(BF16)
    to_next = remote(
        ext.at[pl.ds(mesh, reach)], ext.at[pl.ds(0, reach)], 5, nxt, my
    )
    to_prev = remote(
        ext.at[pl.ds(reach, reach)], ext.at[pl.ds(reach + mesh, reach)], 6, prv, my
    )
    to_next.start()
    to_prev.start()
    to_next.wait()
    to_prev.wait()
    total = dot(rim[...], ext[...]) * fan_m_scale
    neighbour[...] = total
    mid_full[my] = (first[...] + total * jax.nn.sigmoid(total)).astype(BF16)

    def send_mid(c):
        remote(mid_full.at[my], mid_full.at[my], 7, me, c).start()

    chans(send_mid)
    pre = (second[...] * slope(neighbour[...]) * fan_m_scale).astype(BF16)
    rim_grad[...] = dot(rimt[...], pre)
    down = remote(rim_grad.at[pl.ds(0, reach)], halo_high, 8, prv, my)
    up = remote(rim_grad.at[pl.ds(reach + mesh, reach)], halo_low, 9, nxt, my)
    down.start()
    up.start()

    wait_chan(mid_full, 7)
    total = dot(mid_full[0], wd_ref[0:width, :])
    for c in range(1, nc):
        total = total + dot(mid_full[c], wd_ref[c * width : (c + 1) * width, :])
    out_rows[...] = dot(sel[...], total.astype(BF16)).reshape(out_rows.shape)

    def send_rows(peer):
        remote(out_rows.at[peer], slots.at[me], 10, peer, my).start()

    peers(send_rows)
    slots[me] = out_rows[me]

    down.wait()
    up.wait()
    rim_grad[reach : 2 * reach, :] += halo_low[...]
    rim_grad[mesh : mesh + reach, :] += halo_high[...]
    projected = rim_grad[reach : reach + mesh, :].astype(BF16)
    for c in range(nc):
        proj_part[c] = dot_nt(projected, wp_ref[c * width : (c + 1) * width, :]).astype(BF16)

    def send_proj(c):
        remote(proj_part.at[c], proj_recv.at[my], 11, me, c).start()

    chans(send_proj)
    proj_recv[my] = proj_part[my]
    blocks = width // share
    for c in range(nc):
        cut = slice(c * blocks, (c + 1) * blocks)
        grads_a[cut, 0:share, :] = (
            dot_tn(mid_full[c], dgrad[...]).astype(BF16).reshape(blocks, share, width)
        )
        grads_a[cut, share : 2 * share, :] = (
            dot_tn(first_full[c], projected).astype(BF16).reshape(blocks, share, width)
        )

    def send_a(peer):
        remote(grads_a.at[peer], grecv_a.at[me], 12, peer, my).start()

    peers(send_a)
    grecv_a[me] = grads_a[me]

    wait_chan(proj_recv, 11)
    total = second[...]
    for c in range(nc):
        total = total + proj_recv[c].astype(F32)
    sum_grad = (total * slope(gathered[...]) * fan_scale).astype(BF16)
    for c in range(nc):
        cut = slice(c * blocks, (c + 1) * blocks)
        grads_b[cut] = (
            dot_tn(state_full[c], sum_grad).astype(BF16).reshape(blocks, share, width)
        )

    def send_b(peer):
        remote(grads_b.at[peer], grecv_b.at[me], 13, peer, my).start()

    peers(send_b)
    grecv_b[me] = grads_b[me]

    wait_space(slots, 10)
    slots_t[...] = slots[...].reshape(all_slots, width).T.astype(BF16)

    def predict(t, carry):
        for u, buf in enumerate((at_even, at_odd)):
            moved = dot(slots_t[...], buf[t]) * fan_d_scale
            rows = pl.ds(pl.multiple_of((2 * t + u) * CHUNK, CHUNK), CHUNK)
            pred_ref[rows, :] = (grid_ref[rows, :].astype(F32) + moved.T).astype(BF16)
        return carry

    lax.fori_loop(0, steps // 4, predict, 0)

    wait_space(grecv_a, 12)
    wait_space(grecv_b, 13)
    total_a = grecv_a[0].astype(F32)
    total_b = grecv_b[0].astype(F32)
    for s in range(1, ns):
        total_a = total_a + grecv_a[s].astype(F32)
        total_b = total_b + grecv_b[s].astype(F32)
    gout[me, 0 : 2 * share, :] = total_a.astype(BF16)
    gout[me, 2 * share : 3 * share, :] = total_b.astype(BF16)

    def send_out(peer):
        remote(gout.at[me], gout.at[me], 14, peer, my).start()

    peers(send_out)
    lax.fori_loop(steps // 4, steps // 2, predict, 0)
    wait_space(gout, 14)
    whole = gout[...].astype(F32)
    gd_ref[...] = whole[:, 0:share, :].reshape(gd_ref.shape)
    gp_ref[...] = whole[:, share : 2 * share, :].reshape(gp_ref.shape)
    ge_ref[...] = whole[:, 2 * share : 3 * share, :].reshape(ge_ref.shape)

    sent(sendbuf, ns - 1, 0)
    sent(back, ns - 1, 1)
    sent(second_part, nc - 1, 2)
    sent(state_full, nc - 1, 3)
    sent(first_full, nc - 1, 4)
    sent(mid_full, nc - 1, 7)
    sent(out_rows, ns - 1, 10)
    sent(proj_part, nc - 1, 11)
    sent(grads_a, ns - 1, 12)
    sent(grads_b, ns - 1, 13)
    sent(gout, ns - 1, 14)


def local(
    grid_state,
    cotangent,
    encoder_weight,
    processor_weight,
    decoder_weight,
    g2m_send,
    g2m_edges,
    m2g_send,
    m2g_edges,
    m2m_edges,
):
    ns = lax.axis_size("space")
    nc = lax.axis_size("chan")
    grid_rows, width = grid_state.shape
    mesh, fan = g2m_edges.shape
    fan_m = m2m_edges.shape[1]
    fan_d = m2g_edges.shape[1]
    cap = g2m_send.shape[1]
    cap2 = m2g_send.shape[1]
    reach = min(REACH, mesh // 2)
    full = encoder_weight.shape[0]
    share = full // ns
    heads = ns * cap // 128
    halves = grid_rows // CHUNK // 2

    vmem = pl.BlockSpec(memory_space=pltpu.VMEM)
    smem = pl.BlockSpec(memory_space=pltpu.SMEM)
    weight = jax.ShapeDtypeStruct((full, width), F32)
    return tuple(
        pl.pallas_call(
            functools.partial(kernel, (ns, nc, fan, fan_m, fan_d)),
            out_shape=(
                jax.ShapeDtypeStruct(grid_state.shape, BF16),
                weight,
                weight,
                weight,
            ),
            in_specs=[vmem] * 5 + [smem] + [vmem] * 4,
            out_specs=(vmem,) * 4,
            scratch_shapes=[
                pltpu.VMEM((grid_rows, width), F32),
                pltpu.VMEM((cap, width), F32),
                pltpu.VMEM((ns, cap, width), BF16),
                pltpu.VMEM((ns, cap, width), BF16),
                pltpu.VMEM((halves, ns * cap2, CHUNK), BF16),
                pltpu.VMEM((halves, ns * cap2, CHUNK), BF16),
                pltpu.VMEM((mesh // 8, 8 * fan), jnp.int32),
                pltpu.VMEM((mesh // 8, 8 * fan), jnp.int32),
                pltpu.VMEM((heads, mesh, 128), BF16),
                pltpu.VMEM((ns * cap2, width), F32),
                pltpu.VMEM((ns, cap2, width), F32),
                pltpu.VMEM((ns * cap2, mesh), F32),
                pltpu.VMEM((ns * cap2, mesh), BF16),
                pltpu.VMEM((mesh, ns * cap2), BF16),
                pltpu.VMEM((mesh, mesh + 2 * reach), BF16),
                pltpu.VMEM((mesh + 2 * reach, mesh), BF16),
                pltpu.VMEM((mesh, width), BF16),
                pltpu.VMEM((nc, mesh, width), BF16),
                pltpu.VMEM((nc, mesh, width), BF16),
                pltpu.VMEM((mesh, width), F32),
                pltpu.VMEM((mesh, width), F32),
                pltpu.VMEM((nc, mesh, width), BF16),
                pltpu.VMEM((mesh, width), F32),
                pltpu.VMEM((mesh, width), F32),
                pltpu.VMEM((nc, mesh, width), BF16),
                pltpu.VMEM((mesh + 2 * reach, width), BF16),
                pltpu.VMEM((mesh, width), F32),
                pltpu.VMEM((nc, mesh, width), BF16),
                pltpu.VMEM((ns, cap2, width), F32),
                pltpu.VMEM((ns, cap2, width), F32),
                pltpu.VMEM((width, ns * cap2), BF16),
                pltpu.VMEM((mesh + 2 * reach, width), F32),
                pltpu.VMEM((reach, width), F32),
                pltpu.VMEM((reach, width), F32),
                pltpu.VMEM((nc, mesh, width), BF16),
                pltpu.VMEM((nc, mesh, width), BF16),
                pltpu.VMEM((ns, 2 * share, width), BF16),
                pltpu.VMEM((ns, share, width), BF16),
                pltpu.VMEM((ns, 2 * share, width), BF16),
                pltpu.VMEM((ns, share, width), BF16),
                pltpu.VMEM((ns, 3 * share, width), BF16),
                pltpu.SemaphoreType.DMA((15,)),
                pltpu.SemaphoreType.DMA((15,)),
                pltpu.SemaphoreType.DMA((ns,)),
            ],
            compiler_params=pltpu.CompilerParams(
                collective_id=0,
                has_side_effects=True,
                vmem_limit_bytes=56 * 1024 * 1024,
            ),
            cost_estimate=pl.CostEstimate(
                flops=12_000_000_000, bytes_accessed=10_000_000, transcendentals=0
            ),
            name="encode_process_decode",
        )(
            grid_state,
            cotangent,
            encoder_weight,
            processor_weight,
            decoder_weight,
            g2m_send,
            g2m_edges,
            m2g_send.T,
            m2g_edges.T,
            m2m_edges.T,
        )
    )


def solution(mesh):
    placed = (P("space", "chan"),) * 2 + (P(None, "chan"),) * 3 + (P("space", None),) * 5
    return jax.shard_map(
        local,
        mesh=mesh,
        in_specs=placed,
        out_specs=(P("space", "chan"),) + (P(None, "chan"),) * 3,
        check_vma=False,
    )
```

```python
import functools

import jax
import jax.numpy as jnp
from jax import lax
from jax.experimental import pallas as pl
from jax.experimental.pallas import tpu as pltpu
from jax.sharding import PartitionSpec as P

REACH = 160
CHUNK = 1024
MESH = pl.DeviceIdType.MESH
F32 = jnp.float32
BF16 = jnp.bfloat16


def dot(a, b):
    return jnp.dot(a, b, preferred_element_type=F32)


def dot_nt(a, b):
    return lax.dot_general(a, b, (((1,), (1,)), ((), ())), preferred_element_type=F32)


def dot_tn(a, b):
    return lax.dot_general(a, b, (((0,), (0,)), ((), ())), preferred_element_type=F32)


def slope(values):
    sigmoid = jax.nn.sigmoid(values)
    return sigmoid * (1.0 + values * (1.0 - sigmoid))


def row_iota(rows, lanes):
    return lax.broadcasted_iota(jnp.int32, (rows, lanes), 0).astype(F32).astype(BF16)


def ones_where(mask):
    return jnp.where(mask, jnp.ones((), BF16), jnp.zeros((), BF16))


def narrow(row, base):
    return (row - base).astype(F32).astype(BF16)


def kernel(
    sizes,
    grid_ref,
    cot_ref,
    we_ref,
    wp_ref,
    wd_ref,
    send_ref,
    source_ref,
    mesh_send_ref,
    edge_ref,
    near_ref,
    pred_ref,
    ge_ref,
    gp_ref,
    gd_ref,
    grid32,
    stage,
    sendbuf,
    recv,
    at_even,
    at_odd,
    senders,
    key,
    low,
    counts,
    slot_grad,
    back_out,
    back,
    sel32,
    sel,
    selt,
    rim,
    rimt,
    dgrad,
    second_part,
    second_recv,
    second,
    state_sum,
    state_full,
    gathered,
    first,
    first_full,
    ext,
    mid_full,
    out_rows,
    slots,
    slots_t,
    rim_grad,
    halo_low,
    halo_high,
    proj_part,
    proj_recv,
    grads_a,
    grads_b,
    grecv_a,
    grecv_b,
    gout,
    ssem,
    rsem,
    gsem,
):
    ns, nc, fan, fan_m, fan_d = sizes
    me = lax.axis_index("space")
    my = lax.axis_index("chan")
    grid_rows, width = grid_ref.shape
    cap = recv.shape[1]
    mesh = state_sum.shape[0]
    cap2 = mesh_send_ref.shape[1]
    pad2 = back.shape[1]
    reach = halo_low.shape[0]
    share = grads_b.shape[1]
    fan_scale = fan ** (-0.5)
    fan_m_scale = fan_m ** (-0.5)
    fan_d_scale = fan_d ** (-0.5)
    all_slots = ns * cap2
    nxt = lax.rem(me + 1, ns)
    prv = lax.rem(me + ns - 1, ns)

    def remote(src, dst, which, space, chan, rec=None):
        return pltpu.make_async_remote_copy(
            src_ref=src,
            dst_ref=dst,
            send_sem=ssem.at[which],
            recv_sem=rsem.at[which] if rec is None else rec,
            device_id=(space, chan),
            device_id_type=MESH,
        )

    def peers(body):
        def step(k, carry):
            body(lax.rem(me + k, ns))
            return carry

        lax.fori_loop(1, ns, step, 0)

    def chans(body):
        for k in range(1, nc):
            body(lax.rem(my + k, nc))

    def wait_chan(buf, which):
        part = buf.at[pl.ds(0, nc - 1)]
        remote(part, part, which, me, my).wait_recv()

    def wait_space(buf, which):
        part = buf.at[pl.ds(0, ns - 1)]
        remote(part, part, which, me, my).wait_recv()

    def sent(buf, count, which):
        part = buf.at[pl.ds(0, count)]
        remote(part, part, which, me, my).wait_send()

    barrier = pltpu.get_barrier_semaphore()

    def greet(peer):
        pl.semaphore_signal(barrier, inc=1, device_id=(peer, my), device_id_type=MESH)

    peers(greet)

    def greet_chan(c):
        pl.semaphore_signal(barrier, inc=1, device_id=(me, c), device_id_type=MESH)

    chans(greet_chan)

    def widen(i, carry):
        rows = pl.ds(pl.multiple_of(i * CHUNK, CHUNK), CHUNK)
        grid32[rows, :] = grid_ref[rows, :].astype(F32)
        return carry

    lax.fori_loop(0, grid_rows // CHUNK, widen, 0)
    pl.semaphore_wait(barrier, ns + nc - 2)

    lanes = 8 if ns % 8 == 0 else ns

    def pick(peer):
        first_of = (peer // lanes) * (lanes * cap) + lax.rem(peer, lanes) * 128
        for part in range(cap // 128):

            def some(i, carry):
                base = pl.multiple_of(i * 64, 64)
                at = first_of + part * (lanes * 128) + base
                rows = [grid32[pl.ds(send_ref[at + u], 1), :] for u in range(64)]
                for u in range(64):
                    stage[pl.ds(part * 128 + base + u, 1), :] = rows[u]
                return carry

            lax.fori_loop(0, 2, some, 0)

    def pick_and_send(peer):
        pick(peer)
        sendbuf[peer] = stage[...].astype(BF16)
        remote(sendbuf.at[peer], recv.at[me], 0, peer, my, gsem.at[me]).start()

    peers(pick_and_send)
    pick(me)
    recv[me] = stage[...].astype(BF16)

    iota = row_iota(128, 128)
    slot_grad[...] = jnp.zeros(slot_grad.shape, F32)

    steps = grid_rows // CHUNK
    half = all_slots // 2

    def build(buf, at, step, lo, hi):
        start = pl.multiple_of(step * CHUNK, CHUNK)
        rows = edge_ref[:, pl.ds(start, CHUNK)]
        for kb in range(lo // 128, hi // 128):
            cut = [narrow(rows[j : j + 1, :], kb * 128) for j in range(fan_d)]
            for lb in range(CHUNK // 128):
                total = None
                for j in range(fan_d):
                    one = ones_where(iota == cut[j][:, lb * 128 : (lb + 1) * 128])
                    total = one if total is None else total + one
                buf[at, kb * 128 : (kb + 1) * 128, lb * 128 : (lb + 1) * 128] = total

    def spread(buf, at, step, lo, hi):
        rows = pl.ds(pl.multiple_of(step * CHUNK, CHUNK), CHUNK)
        slot_grad[lo:hi, :] += dot(buf[at, lo:hi, :], cot_ref[rows, :])

    cuts = [(0, half), (half, all_slots)] if half % 128 == 0 else [(0, all_slots)]
    build(at_even, 0, 0, 0, all_slots)

    def edge_step(t, carry):
        for lo, hi in cuts:
            spread(at_even, t, 2 * t, lo, hi)
            build(at_odd, t, 2 * t + 1, lo, hi)
        for lo, hi in cuts:
            spread(at_odd, t, 2 * t + 1, lo, hi)
            build(at_even, t + 1, 2 * t + 2, lo, hi)
        return carry

    last = steps // 2 - 1
    lax.fori_loop(0, last, edge_step, 0)
    for lo, hi in cuts:
        spread(at_even, last, 2 * last, lo, hi)
        build(at_odd, last, 2 * last + 1, lo, hi)
    spread(at_odd, last, 2 * last + 1, 0, all_slots)
    back_out[:, 0:cap2, :] = (
        (slot_grad[...] * fan_d_scale).reshape(ns, cap2, width).astype(BF16)
    )
    back_out[:, cap2:pad2, :] = jnp.zeros((ns, pad2 - cap2, width), BF16)

    def send_back(peer):
        remote(back_out.at[peer], back.at[me], 1, peer, my).start()

    peers(send_back)
    back[me] = back_out[me]

    octets = mesh // 8
    senders[...] = source_ref[...].astype(F32).T
    parts = [
        senders[pl.ds(u, octets, stride=8), :].astype(jnp.int32) for u in range(8)
    ]
    key[...] = jnp.concatenate([(part // cap) * 8 + u for u, part in enumerate(parts)], axis=1)
    low[...] = jnp.concatenate([part % cap for part in parts], axis=1)
    big = row_iota(128, key.shape[1])

    def one_hot(row, rows):
        step = min(rows, 128)
        return jnp.concatenate(
            [ones_where(big[0:step] == narrow(row, base)) for base in range(0, rows, step)], axis=0
        )

    def count_step(g, carry):
        found = []
        for u in range(2):
            row = pl.ds(2 * g + u, 1)
            left = one_hot(key[row, :], 8 * ns)
            found.append(dot_nt(left, one_hot(low[row, :], cap)).reshape(ns, 8, cap))
        rows = pl.ds(pl.multiple_of(g * 16, 16), 16)
        counts[:, rows, :] = jnp.concatenate(found, axis=1).astype(BF16)
        return carry

    lax.fori_loop(0, mesh // 16, count_step, 0, unroll=5 if mesh % 80 == 0 else 1)

    node = lax.broadcasted_iota(jnp.int32, near_ref.shape, 1)
    span = ns * mesh
    offset = near_ref[...] - me * mesh - node + reach
    offset = jnp.where(offset < 0, offset + span, offset)
    offset = jnp.where(offset >= span, offset - span, offset) + node
    rows_iota = lax.broadcasted_iota(jnp.int32, rimt.shape, 0)
    total = jnp.zeros(rimt.shape, F32)
    for j in range(fan_m):
        total = total + jnp.where(rows_iota == offset[j : j + 1, :], 1.0, 0.0)
    rimt[...] = total.astype(BF16)
    rim[...] = total.T.astype(BF16)
    mesh_send = mesh_send_ref[...].astype(F32).T
    lane_iota = lax.broadcasted_iota(jnp.int32, (cap2, mesh), 1).astype(F32)
    for p in range(ns):
        hot = jnp.where(lane_iota == mesh_send[:, p : p + 1], 1.0, 0.0)
        sel32[p * pad2 : p * pad2 + cap2, :] = hot
        sel32[p * pad2 + cap2 : (p + 1) * pad2, :] = jnp.zeros((pad2 - cap2, mesh), F32)
    sel[...] = sel32[...].astype(BF16)
    selt[...] = sel32[...].T.astype(BF16)

    quad = 4
    quads = ns // quad

    def absorb(first_source):
        total = dot(counts[first_source], recv[first_source])
        for u in range(1, quad):
            total = total + dot(counts[first_source + u], recv[first_source + u])
        return total

    def arrived(source):
        remote(recv.at[source], recv.at[source], 0, me, my, gsem.at[source]).wait_recv()

    state_sum[...] = jnp.zeros(state_sum.shape, F32)

    def absorb_step(k, carry):
        base = lax.rem(me // quad + quads - k, quads) * quad
        for u in range(quad):
            arrived(base + u)
        state_sum[...] += absorb(base)
        return carry

    lax.fori_loop(1, quads, absorb_step, 0)
    own = (me // quad) * quad
    for u in range(1, quad):
        arrived(own + lax.rem(me + u, quad))
    state_full[my] = (state_sum[...] + absorb(own)).astype(BF16)

    def send_state(c):
        remote(state_full.at[my], state_full.at[my], 3, me, c).start()

    chans(send_state)

    wait_space(back, 1)
    dgrad[...] = dot(selt[...], back[...].reshape(ns * pad2, width)).astype(BF16)
    for c in range(nc):
        second_part[c] = dot_nt(dgrad[...], wd_ref[c * width : (c + 1) * width, :]).astype(BF16)

    wait_chan(state_full, 3)
    total = dot(state_full[0], we_ref[0:width, :])
    for c in range(1, nc):
        total = total + dot(state_full[c], we_ref[c * width : (c + 1) * width, :])
    total = total * fan_scale
    gathered[...] = total
    first_full[my] = (total * jax.nn.sigmoid(total)).astype(BF16)

    def send_first(c):
        remote(first_full.at[my], first_full.at[my], 4, me, c).start()

    chans(send_first)

    def send_second(c):
        remote(second_part.at[c], second_recv.at[my], 2, me, c).start()

    chans(send_second)
    second_recv[my] = second_part[my]
    first[...] = first_full[my].astype(F32)
    gathered[...] = slope(gathered[...]) * fan_scale
    wait_chan(first_full, 4)
    total = dot(first_full[0], wp_ref[0:width, :])
    for c in range(1, nc):
        total = total + dot(first_full[c], wp_ref[c * width : (c + 1) * width, :])
    ext[reach : reach + mesh, :] = total.astype(BF16)
    to_next = remote(ext.at[pl.ds(mesh, reach)], ext.at[pl.ds(0, reach)], 5, nxt, my)
    to_prev = remote(
        ext.at[pl.ds(reach, reach)], ext.at[pl.ds(reach + mesh, reach)], 6, prv, my
    )
    to_next.start()
    to_prev.start()
    wait_chan(second_recv, 2)
    total = second_recv[0].astype(F32)
    for c in range(1, nc):
        total = total + second_recv[c].astype(F32)
    second[...] = total
    to_next.wait()
    to_prev.wait()
    total = dot(rim[...], ext[...]) * fan_m_scale
    sigmoid = jax.nn.sigmoid(total)
    mid_full[my] = (first[...] + total * sigmoid).astype(BF16)

    def send_mid(c):
        remote(mid_full.at[my], mid_full.at[my], 7, me, c).start()

    chans(send_mid)
    slant = sigmoid * (1.0 + total * (1.0 - sigmoid))
    pre = (second[...] * slant * fan_m_scale).astype(BF16)
    rim_grad[...] = dot(rimt[...], pre)
    down = remote(rim_grad.at[pl.ds(0, reach)], halo_high, 8, prv, my)
    up = remote(rim_grad.at[pl.ds(reach + mesh, reach)], halo_low, 9, nxt, my)
    down.start()
    up.start()
    down.wait()
    up.wait()
    rim_grad[reach : 2 * reach, :] += halo_low[...]
    rim_grad[mesh : mesh + reach, :] += halo_high[...]
    projected = rim_grad[reach : reach + mesh, :].astype(BF16)
    for c in range(nc):
        proj_part[c] = dot_nt(projected, wp_ref[c * width : (c + 1) * width, :]).astype(BF16)

    def send_proj(c):
        remote(proj_part.at[c], proj_recv.at[my], 11, me, c).start()

    chans(send_proj)
    proj_recv[my] = proj_part[my]

    wait_chan(mid_full, 7)
    total = dot(mid_full[0], wd_ref[0:width, :])
    for c in range(1, nc):
        total = total + dot(mid_full[c], wd_ref[c * width : (c + 1) * width, :])
    out_rows[...] = dot(sel[...], total.astype(BF16)).astype(BF16).reshape(out_rows.shape)

    def send_rows(peer):
        remote(out_rows.at[peer], slots.at[me], 10, peer, my).start()

    peers(send_rows)
    slots[me] = out_rows[me]
    blocks = width // share

    def split(grad):
        return grad.astype(BF16).reshape(blocks, share, width)

    for c in range(nc):
        cut = slice(c * blocks, (c + 1) * blocks)
        grads_a[cut, 0:share, :] = split(dot_tn(mid_full[c], dgrad[...]))
        grads_a[cut, share : 2 * share, :] = split(dot_tn(first_full[c], projected))

    wait_chan(proj_recv, 11)
    total = second[...]
    for c in range(nc):
        total = total + proj_recv[c].astype(F32)
    sum_grad = (total * gathered[...]).astype(BF16)
    for c in range(nc):
        grads_b[c * blocks : (c + 1) * blocks] = split(dot_tn(state_full[c], sum_grad))

    def send_grads(peer):
        remote(grads_b.at[peer], grecv_b.at[me], 13, peer, my).start()
        remote(grads_a.at[peer], grecv_a.at[me], 12, peer, my).start()

    peers(send_grads)
    grecv_a[me] = grads_a[me]
    grecv_b[me] = grads_b[me]

    wait_space(slots, 10)
    rows = slots[...].astype(F32)[:, 0:cap2, :].reshape(all_slots, width)
    slots_t[...] = rows.T.astype(BF16)

    def predict(t, carry):
        for u, buf in enumerate((at_even, at_odd)):
            moved = dot(slots_t[...], buf[t]) * fan_d_scale
            rows = pl.ds(pl.multiple_of((2 * t + u) * CHUNK, CHUNK), CHUNK)
            pred_ref[rows, :] = (grid_ref[rows, :].astype(F32) + moved.T).astype(BF16)
        return carry

    lax.fori_loop(0, steps // 4, predict, 0)

    wait_space(grecv_a, 12)
    wait_space(grecv_b, 13)
    total_a = grecv_a[0].astype(F32)
    total_b = grecv_b[0].astype(F32)
    for s in range(1, ns):
        total_a = total_a + grecv_a[s].astype(F32)
        total_b = total_b + grecv_b[s].astype(F32)
    gout[me, 0 : 2 * share, :] = total_a.astype(BF16)
    gout[me, 2 * share : 3 * share, :] = total_b.astype(BF16)

    def send_out(peer):
        remote(gout.at[me], gout.at[me], 14, peer, my).start()

    peers(send_out)
    lax.fori_loop(steps // 4, steps // 2, predict, 0)
    wait_space(gout, 14)
    whole = gout[...].astype(F32)
    gd_ref[...] = whole[:, 0:share, :].reshape(gd_ref.shape)
    gp_ref[...] = whole[:, share : 2 * share, :].reshape(gp_ref.shape)
    ge_ref[...] = whole[:, 2 * share : 3 * share, :].reshape(ge_ref.shape)

    sent(sendbuf, ns - 1, 0)
    sent(back, ns - 1, 1)
    sent(second_part, nc - 1, 2)
    sent(state_full, nc - 1, 3)
    sent(first_full, nc - 1, 4)
    sent(mid_full, nc - 1, 7)
    sent(out_rows, ns - 1, 10)
    sent(proj_part, nc - 1, 11)
    sent(grads_a, ns - 1, 12)
    sent(grads_b, ns - 1, 13)
    sent(gout, ns - 1, 14)


def local(
    grid_state,
    cotangent,
    encoder_weight,
    processor_weight,
    decoder_weight,
    g2m_send,
    g2m_edges,
    m2g_send,
    m2g_edges,
    m2m_edges,
):
    ns = lax.axis_size("space")
    nc = lax.axis_size("chan")
    grid_rows, width = grid_state.shape
    mesh, fan = g2m_edges.shape
    fan_m = m2m_edges.shape[1]
    fan_d = m2g_edges.shape[1]
    cap = g2m_send.shape[1]
    cap2 = m2g_send.shape[1]
    reach = min(REACH, mesh // 2)
    full = encoder_weight.shape[0]
    share = full // ns
    pad2 = (cap2 + 15) // 16 * 16
    tall = 8 if ns % 8 == 0 else ns
    send = g2m_send.reshape(ns // tall, tall, cap // 128, 128).transpose(0, 2, 1, 3).reshape(-1)
    halves = grid_rows // CHUNK // 2

    vmem = pl.BlockSpec(memory_space=pltpu.VMEM)
    smem = pl.BlockSpec(memory_space=pltpu.SMEM)
    weight = jax.ShapeDtypeStruct((full, width), F32)
    return tuple(
        pl.pallas_call(
            functools.partial(kernel, (ns, nc, fan, fan_m, fan_d)),
            out_shape=(
                jax.ShapeDtypeStruct(grid_state.shape, BF16),
                weight,
                weight,
                weight,
            ),
            in_specs=[vmem] * 5 + [smem] + [vmem] * 4,
            out_specs=(vmem,) * 4,
            scratch_shapes=[
                pltpu.VMEM((grid_rows, width), F32),
                pltpu.VMEM((cap, width), F32),
                pltpu.VMEM((ns, cap, width), BF16),
                pltpu.VMEM((ns, cap, width), BF16),
                pltpu.VMEM((halves, ns * cap2, CHUNK), BF16),
                pltpu.VMEM((halves, ns * cap2, CHUNK), BF16),
                pltpu.VMEM((mesh, fan), F32),
                pltpu.VMEM((mesh // 8, 8 * fan), jnp.int32),
                pltpu.VMEM((mesh // 8, 8 * fan), jnp.int32),
                pltpu.VMEM((ns, mesh, cap), BF16),
                pltpu.VMEM((ns * cap2, width), F32),
                pltpu.VMEM((ns, pad2, width), BF16),
                pltpu.VMEM((ns, pad2, width), BF16),
                pltpu.VMEM((ns * pad2, mesh), F32),
                pltpu.VMEM((ns * pad2, mesh), BF16),
                pltpu.VMEM((mesh, ns * pad2), BF16),
                pltpu.VMEM((mesh, mesh + 2 * reach), BF16),
                pltpu.VMEM((mesh + 2 * reach, mesh), BF16),
                pltpu.VMEM((mesh, width), BF16),
                pltpu.VMEM((nc, mesh, width), BF16),
                pltpu.VMEM((nc, mesh, width), BF16),
                pltpu.VMEM((mesh, width), F32),
                pltpu.VMEM((mesh, width), F32),
                pltpu.VMEM((nc, mesh, width), BF16),
                pltpu.VMEM((mesh, width), F32),
                pltpu.VMEM((mesh, width), F32),
                pltpu.VMEM((nc, mesh, width), BF16),
                pltpu.VMEM((mesh + 2 * reach, width), BF16),
                pltpu.VMEM((nc, mesh, width), BF16),
                pltpu.VMEM((ns, pad2, width), BF16),
                pltpu.VMEM((ns, pad2, width), BF16),
                pltpu.VMEM((width, ns * cap2), BF16),
                pltpu.VMEM((mesh + 2 * reach, width), F32),
                pltpu.VMEM((reach, width), F32),
                pltpu.VMEM((reach, width), F32),
                pltpu.VMEM((nc, mesh, width), BF16),
                pltpu.VMEM((nc, mesh, width), BF16),
                pltpu.VMEM((ns, 2 * share, width), BF16),
                pltpu.VMEM((ns, share, width), BF16),
                pltpu.VMEM((ns, 2 * share, width), BF16),
                pltpu.VMEM((ns, share, width), BF16),
                pltpu.VMEM((ns, 3 * share, width), BF16),
                pltpu.SemaphoreType.DMA((15,)),
                pltpu.SemaphoreType.DMA((15,)),
                pltpu.SemaphoreType.DMA((ns,)),
            ],
            compiler_params=pltpu.CompilerParams(
                collective_id=0,
                has_side_effects=True,
                vmem_limit_bytes=56 * 1024 * 1024,
            ),
            cost_estimate=pl.CostEstimate(
                flops=12_000_000_000, bytes_accessed=10_000_000, transcendentals=0
            ),
            name="encode_process_decode",
        )(
            grid_state,
            cotangent,
            encoder_weight,
            processor_weight,
            decoder_weight,
            send,
            g2m_edges.T,
            m2g_send,
            m2g_edges.T,
            m2m_edges.T,
        )
    )


def solution(mesh):
    placed = (P("space", "chan"),) * 2 + (P(None, "chan"),) * 3 + (P("space", None),) * 5
    return jax.shard_map(
        local,
        mesh=mesh,
        in_specs=placed,
        out_specs=(P("space", "chan"),) + (P(None, "chan"),) * 3,
        check_vma=False,
    )
```

```python
import functools

import jax
import jax.numpy as jnp
from jax import lax
from jax.experimental import pallas as pl
from jax.experimental.pallas import tpu as pltpu
from jax.sharding import PartitionSpec as P

REACH = 160
CHUNK = 1024
MESH = pl.DeviceIdType.MESH
F32 = jnp.float32
BF16 = jnp.bfloat16


def dot(a, b):
    return jnp.dot(a, b, preferred_element_type=F32)


def dot_nt(a, b):
    return lax.dot_general(a, b, (((1,), (1,)), ((), ())), preferred_element_type=F32)


def dot_tn(a, b):
    return lax.dot_general(a, b, (((0,), (0,)), ((), ())), preferred_element_type=F32)


def slope(values):
    sigmoid = jax.nn.sigmoid(values)
    return sigmoid * (1.0 + values * (1.0 - sigmoid))


def row_iota(rows, lanes):
    return lax.broadcasted_iota(jnp.int32, (rows, lanes), 0).astype(F32).astype(BF16)


def ones_where(mask):
    return jnp.where(mask, jnp.ones((), BF16), jnp.zeros((), BF16))


def narrow(row, base):
    return (row - base).astype(F32).astype(BF16)


def kernel(
    sizes,
    grid_hbm,
    cot_hbm,
    we_hbm,
    wp_hbm,
    wd_hbm,
    send_ref,
    source_ref,
    mesh_send_ref,
    edge_ref,
    near_ref,
    pred_ref,
    ge_ref,
    gp_ref,
    gd_ref,
    grid_ref,
    cot_ref,
    we_all,
    wp_all,
    wd_ref,
    grid32,
    stage,
    sendbuf,
    recv,
    at_even,
    at_odd,
    senders,
    key,
    low,
    counts,
    slot_grad,
    back_out,
    back,
    sel32,
    sel,
    selt,
    rim,
    rimt,
    dgrad,
    second_part,
    second_recv,
    second,
    state_sum,
    state_full,
    state_rows,
    gathered,
    first_rows,
    proj_rows,
    ext,
    mid_full,
    out_rows,
    slots,
    slots_t,
    rim_grad,
    halo_low,
    halo_high,
    proj_part,
    proj_recv,
    grads_a,
    grads_b,
    grecv_a,
    grecv_b,
    gout_a,
    gout_b,
    ssem,
    rsem,
    gsem,
    isem,
):
    ns, nc, fan, fan_m, fan_d = sizes
    me = lax.axis_index("space")
    my = lax.axis_index("chan")
    grid_rows, width = grid_ref.shape
    cap = recv.shape[1]
    mesh = state_sum.shape[0]
    cap2 = mesh_send_ref.shape[1]
    pad2 = back.shape[1]
    reach = halo_low.shape[0]
    share = grads_b.shape[1]
    fan_scale = fan ** (-0.5)
    fan_m_scale = fan_m ** (-0.5)
    fan_d_scale = fan_d ** (-0.5)
    all_slots = ns * cap2
    nxt = lax.rem(me + 1, ns)
    prv = lax.rem(me + ns - 1, ns)

    def remote(src, dst, which, space, chan, rec=None):
        return pltpu.make_async_remote_copy(
            src_ref=src,
            dst_ref=dst,
            send_sem=ssem.at[which],
            recv_sem=rsem.at[which] if rec is None else rec,
            device_id=(space, chan),
            device_id_type=MESH,
        )

    side = 4 if ns == 32 else 1

    def at_distance(k, sign):
        if side == 1:
            return lax.rem(me + ns + sign * k, ns)
        along_x = lax.rem(me // 8 + side + sign * lax.rem(k, side), side)
        along_y = lax.rem(me // 2 + side + sign * lax.rem(k // side, side), side)
        return along_x * 8 + along_y * 2 + lax.rem(me + k // 16, 2)

    def peers(body, lo=1, hi=ns):
        def step(k, carry):
            body(at_distance(k, 1))
            return carry

        lax.fori_loop(lo, hi, step, 0)

    def chans(body):
        for k in range(1, nc):
            body(lax.rem(my + k, nc))

    def wait_chan(buf, which):
        part = buf.at[pl.ds(0, nc - 1)]
        remote(part, part, which, me, my).wait_recv()

    def wait_space(buf, which):
        part = buf.at[pl.ds(0, ns - 1)]
        remote(part, part, which, me, my).wait_recv()

    def sent(buf, count, which):
        part = buf.at[pl.ds(0, count)]
        remote(part, part, which, me, my).wait_send()

    loads = [
        pltpu.make_async_copy(src, dst, isem.at[i])
        for i, (src, dst) in enumerate(
            (
                (grid_hbm, grid_ref),
                (cot_hbm, cot_ref),
                (we_hbm, we_all.at[my]),
                (wp_hbm, wp_all.at[my]),
                (wd_hbm, wd_ref),
            )
        )
    ]
    loads[0].start()
    barrier = pltpu.get_barrier_semaphore()

    def greet(peer):
        pl.semaphore_signal(barrier, inc=1, device_id=(peer, my), device_id_type=MESH)

    peers(greet)

    def greet_chan(c):
        pl.semaphore_signal(barrier, inc=1, device_id=(me, c), device_id_type=MESH)

    chans(greet_chan)

    def greet_beside(c):
        for space in (nxt, prv):
            pl.semaphore_signal(barrier, inc=1, device_id=(space, c), device_id_type=MESH)

    chans(greet_beside)

    for load in loads[1:]:
        load.start()
    loads[0].wait()

    def widen(i, carry):
        rows = pl.ds(pl.multiple_of(i * CHUNK, CHUNK), CHUNK)
        grid32[rows, :] = grid_ref[rows, :].astype(F32)
        return carry

    lax.fori_loop(0, grid_rows // CHUNK, widen, 0)

    lanes = 8 if ns % 8 == 0 else ns

    def pick(peer):
        first_of = (peer // lanes) * (lanes * cap) + lax.rem(peer, lanes) * 128
        for part in range(cap // 128):

            def some(i, carry):
                base = pl.multiple_of(i * 64, 64)
                at = first_of + part * (lanes * 128) + base
                rows = [grid32[pl.ds(send_ref[at + u], 1), :] for u in range(64)]
                for u in range(64):
                    stage[pl.ds(part * 128 + base + u, 1), :] = rows[u]
                return carry

            lax.fori_loop(0, 2, some, 0)

    def pick_for(peer):
        pick(peer)
        sendbuf[peer] = stage[...].astype(BF16)

    def send_picked(peer):
        remote(sendbuf.at[peer], recv.at[me], 0, peer, my, gsem.at[me]).start()

    def pick_and_send(peer):
        pick_for(peer)
        send_picked(peer)

    early = ns // 2
    peers(pick_for, 1, early)

    mesh_send = mesh_send_ref[...].astype(F32).T
    lane_iota = lax.broadcasted_iota(jnp.int32, (cap2, mesh), 1).astype(F32)
    for p in range(ns):
        hot = jnp.where(lane_iota == mesh_send[:, p : p + 1], 1.0, 0.0)
        sel32[p * pad2 : p * pad2 + cap2, :] = hot
        if pad2 > cap2:
            sel32[p * pad2 + cap2 : (p + 1) * pad2, :] = jnp.zeros((pad2 - cap2, mesh), F32)
    sel[...] = sel32[...].astype(BF16)
    selt[...] = sel32[...].T.astype(BF16)

    pl.semaphore_wait(barrier, ns - 1 + 3 * (nc - 1))
    peers(send_picked, 1, early)
    for load in loads[1:]:
        load.wait()

    def send_weights(c):
        remote(we_all.at[my], we_all.at[my], 16, me, c).start()
        remote(wp_all.at[my], wp_all.at[my], 17, me, c).start()

    chans(send_weights)

    iota = row_iota(128, 128)
    slot_grad[...] = jnp.zeros(slot_grad.shape, F32)

    steps = grid_rows // CHUNK
    half = all_slots // 2

    def build(buf, at, step, lo, hi):
        start = pl.multiple_of(step * CHUNK, CHUNK)
        rows = edge_ref[:, pl.ds(start, CHUNK)]
        for kb in range(lo // 128, hi // 128):
            cut = [narrow(rows[j : j + 1, :], kb * 128) for j in range(fan_d)]
            for lb in range(CHUNK // 128):
                total = None
                for j in range(fan_d):
                    one = ones_where(iota == cut[j][:, lb * 128 : (lb + 1) * 128])
                    total = one if total is None else total + one
                buf[at, kb * 128 : (kb + 1) * 128, lb * 128 : (lb + 1) * 128] = total

    def spread(buf, at, step, lo, hi):
        rows = pl.ds(pl.multiple_of(step * CHUNK, CHUNK), CHUNK)
        slot_grad[lo:hi, :] += dot(buf[at, lo:hi, :], cot_ref[rows, :])

    cuts = [(0, half), (half, all_slots)] if half % 128 == 0 else [(0, all_slots)]
    build(at_even, 0, 0, 0, all_slots)

    def edge_step(t, carry):
        for lo, hi in cuts:
            spread(at_even, t, 2 * t, lo, hi)
            build(at_odd, t, 2 * t + 1, lo, hi)
        for lo, hi in cuts:
            spread(at_odd, t, 2 * t + 1, lo, hi)
            build(at_even, t + 1, 2 * t + 2, lo, hi)
        return carry

    last = steps // 2 - 1
    lax.fori_loop(0, last, edge_step, 0)
    for lo, hi in cuts:
        spread(at_even, last, 2 * last, lo, hi)
        build(at_odd, last, 2 * last + 1, lo, hi)
    spread(at_odd, last, 2 * last + 1, 0, all_slots)
    back_out[:, 0:cap2, :] = (
        (slot_grad[...] * fan_d_scale).reshape(ns, cap2, width).astype(BF16)
    )
    if pad2 > cap2:
        back_out[:, cap2:pad2, :] = jnp.zeros((ns, pad2 - cap2, width), BF16)

    def send_back(peer):
        remote(back_out.at[peer], back.at[me], 1, peer, my).start()

    peers(send_back)
    back[me] = back_out[me]

    peers(pick_and_send, early, ns)
    pick(me)
    recv[me] = stage[...].astype(BF16)

    octets = mesh // 8
    senders[...] = source_ref[...].astype(F32).T
    parts = [
        senders[pl.ds(u, octets, stride=8), :].astype(jnp.int32) for u in range(8)
    ]
    key[...] = jnp.concatenate([(part // cap) * 8 + u for u, part in enumerate(parts)], axis=1)
    low[...] = jnp.concatenate([part % cap for part in parts], axis=1)
    big = row_iota(128, key.shape[1])

    def one_hot(row, rows):
        step = min(rows, 128)
        return jnp.concatenate(
            [ones_where(big[0:step] == narrow(row, base)) for base in range(0, rows, step)], axis=0
        )

    def count_step(g, carry):
        found = []
        for u in range(2):
            row = pl.ds(2 * g + u, 1)
            left = one_hot(key[row, :], 8 * ns)
            found.append(dot_nt(left, one_hot(low[row, :], cap)).reshape(ns, 8, cap))
        rows = pl.ds(pl.multiple_of(g * 16, 16), 16)
        counts[:, rows, :] = jnp.concatenate(found, axis=1).astype(BF16)
        return carry

    lax.fori_loop(0, mesh // 16, count_step, 0, unroll=5 if mesh % 80 == 0 else 1)

    wait_space(back, 1)
    dgrad[...] = dot(selt[...], back[...].reshape(ns * pad2, width)).astype(BF16)
    for c in range(nc):
        second_part[c] = dot_nt(dgrad[...], wd_ref[c * width : (c + 1) * width, :]).astype(BF16)

    def send_second(c):
        remote(second_part.at[c], second_recv.at[my], 2, me, c).start()

    chans(send_second)
    second_recv[my] = second_part[my]
    def absorb(k, waits):
        total = None
        for u in range(4):
            source = at_distance(4 * k + u, -1)
            if waits or u > 0:
                remote(recv.at[source], recv.at[source], 0, me, my, gsem.at[source]).wait_recv()
            term = dot(counts[source], recv[source])
            total = term if total is None else total + term
        return total

    state_sum[...] = absorb(0, False)

    def absorb_step(k, carry):
        state_sum[...] += absorb(k, True)
        return carry

    lax.fori_loop(1, ns // 4, absorb_step, 0)
    state_full[my] = state_sum[...].astype(BF16)

    piece = mesh // nc
    own_piece = pl.ds(pl.multiple_of(my * piece, 16), piece)

    def send_rows_of_sum(c):
        rows = pl.ds(pl.multiple_of(c * piece, 16), piece)
        remote(state_full.at[my, rows], state_rows.at[my], 18, me, c).start()

    chans(send_rows_of_sum)
    state_rows[my] = state_full[my, own_piece, :]

    def send_state(c):
        remote(state_full.at[my], state_full.at[my], 3, me, c).start()

    chans(send_state)

    node = lax.broadcasted_iota(jnp.int32, near_ref.shape, 1)
    span = ns * mesh
    offset = near_ref[...] - me * mesh - node + reach
    offset = jnp.where(offset < 0, offset + span, offset)
    offset = jnp.where(offset >= span, offset - span, offset) + node
    rows_iota = lax.broadcasted_iota(jnp.int32, rimt.shape, 0)
    total = jnp.zeros(rimt.shape, F32)
    for j in range(fan_m):
        total = total + jnp.where(rows_iota == offset[j : j + 1, :], 1.0, 0.0)
    rimt[...] = total.astype(BF16)
    rim[...] = total.T.astype(BF16)
    wait_chan(we_all, 16)
    wait_chan(wp_all, 17)
    wait_chan(state_rows, 18)
    whole = jnp.concatenate([state_rows[c] for c in range(nc)], axis=1)
    total = jnp.concatenate([dot(whole, we_all[c]) for c in range(nc)], axis=1) * fan_scale
    latent = (total * jax.nn.sigmoid(total)).astype(BF16)
    first_rows[my] = latent
    for c in range(nc):
        proj_rows[c] = dot(latent, wp_all[c]).astype(BF16)
    upper = my >= nc // 2
    beside = jnp.where(upper, nxt, prv)
    inner = pl.ds(pl.multiple_of(reach + my * piece, 16), piece)
    outer = pl.ds(
        pl.multiple_of(jnp.where(upper, my * piece - (mesh - reach), reach + mesh + my * piece), 16),
        piece,
    )

    def send_projected(c):
        remote(proj_rows.at[c], ext.at[inner], 19, me, c).start()

    def send_beside(c):
        remote(proj_rows.at[c], ext.at[outer], 19, beside, c).start()

    chans(send_projected)
    send_beside(my)
    chans(send_beside)
    ext[inner, :] = proj_rows[my]

    def send_first(c):
        remote(first_rows.at[my], first_rows.at[my], 4, me, c).start()

    chans(send_first)

    wait_chan(second_recv, 2)
    total = second_recv[0].astype(F32)
    for c in range(1, nc):
        total = total + second_recv[c].astype(F32)
    second[...] = total
    wait_chan(state_full, 3)
    total = dot(state_full[0], we_all[my, 0:width, :])
    for c in range(1, nc):
        total = total + dot(state_full[c], we_all[my, c * width : (c + 1) * width, :])
    gathered[...] = slope(total * fan_scale) * fan_scale
    seven = ext.at[pl.ds(0, (2 * nc - 1) * piece)]
    remote(seven, seven, 19, me, my).wait_recv()
    total = dot(rim[...], ext[...]) * fan_m_scale
    sigmoid = jax.nn.sigmoid(total)
    silu = total * sigmoid
    slant = sigmoid * (1.0 + total * (1.0 - sigmoid))
    pre = (second[...] * slant * fan_m_scale).astype(BF16)
    rim_grad[...] = dot(rimt[...], pre)
    down = remote(rim_grad.at[pl.ds(0, reach)], halo_high, 8, prv, my)
    up = remote(rim_grad.at[pl.ds(reach + mesh, reach)], halo_low, 9, nxt, my)
    down.start()
    up.start()
    wait_chan(first_rows, 4)
    own_lanes = pl.ds(pl.multiple_of(my * width, width), width)
    first = first_rows[:, :, own_lanes].reshape(mesh, width).astype(F32)
    mid_full[my] = (first + silu).astype(BF16)

    def send_mid(c):
        remote(mid_full.at[my], mid_full.at[my], 7, me, c).start()

    chans(send_mid)
    down.wait()
    up.wait()
    rim_grad[reach : 2 * reach, :] += halo_low[...]
    rim_grad[mesh : mesh + reach, :] += halo_high[...]
    projected = rim_grad[reach : reach + mesh, :].astype(BF16)
    for c in range(nc):
        proj_part[c] = dot_nt(projected, wp_all[my, c * width : (c + 1) * width, :]).astype(BF16)

    def send_proj(c):
        remote(proj_part.at[c], proj_recv.at[my], 11, me, c).start()

    chans(send_proj)
    proj_recv[my] = proj_part[my]

    wait_chan(mid_full, 7)
    total = dot(mid_full[0], wd_ref[0:width, :])
    for c in range(1, nc):
        total = total + dot(mid_full[c], wd_ref[c * width : (c + 1) * width, :])
    out_rows[...] = dot(sel[...], total.astype(BF16)).astype(BF16).reshape(out_rows.shape)

    def send_rows(peer):
        remote(out_rows.at[peer], slots.at[me], 10, peer, my).start()

    peers(send_rows)
    slots[me] = out_rows[me]
    blocks = width // share

    def split(grad):
        return grad.astype(BF16).reshape(blocks, share, width)

    for c in range(nc):
        cut = slice(c * blocks, (c + 1) * blocks)
        grads_a[cut, 0:share, :] = split(dot_tn(mid_full[c], dgrad[...]))
        grads_a[cut, share : 2 * share, :] = split(
            dot_tn(first_rows[:, :, c * width : (c + 1) * width].reshape(mesh, width), projected)
        )

    def send_a(peer):
        remote(grads_a.at[peer], grecv_a.at[me], 12, peer, my).start()

    peers(send_a)
    grecv_a[me] = grads_a[me]
    wait_chan(proj_recv, 11)
    total = second[...]
    for c in range(nc):
        total = total + proj_recv[c].astype(F32)
    sum_grad = (total * gathered[...]).astype(BF16)
    for c in range(nc):
        grads_b[c * blocks : (c + 1) * blocks] = split(dot_tn(state_full[c], sum_grad))

    def send_b(peer):
        remote(grads_b.at[peer], grecv_b.at[me], 13, peer, my).start()

    peers(send_b)
    grecv_b[me] = grads_b[me]

    wait_space(slots, 10)
    rows = slots[...].astype(F32)[:, 0:cap2, :].reshape(all_slots, width)
    slots_t[...] = rows.T.astype(BF16)

    def predict(t, carry):
        for u, buf in enumerate((at_even, at_odd)):
            moved = dot(slots_t[...], buf[t]) * fan_d_scale
            rows = pl.ds(pl.multiple_of((2 * t + u) * CHUNK, CHUNK), CHUNK)
            pred_ref[rows, :] = (grid_ref[rows, :].astype(F32) + moved.T).astype(BF16)
        return carry

    def gather_sum(got, whole):
        total = got[0].astype(F32)
        for source in range(1, ns):
            total = total + got[source].astype(F32)
        whole[me] = total.astype(BF16)

    def send_out_a(peer):
        remote(gout_a.at[me], gout_a.at[me], 14, peer, my).start()

    def send_out_b(peer):
        remote(gout_b.at[me], gout_b.at[me], 15, peer, my).start()

    quarter = max(steps // 8, 1)
    lax.fori_loop(0, quarter, predict, 0)
    wait_space(grecv_b, 13)
    gather_sum(grecv_b, gout_b)
    peers(send_out_b)
    wait_space(grecv_a, 12)
    gather_sum(grecv_a, gout_a)
    peers(send_out_a)
    lax.fori_loop(quarter, steps // 2, predict, 0)
    wait_space(gout_b, 15)
    ge_ref[...] = gout_b[...].astype(F32).reshape(ge_ref.shape)
    wait_space(gout_a, 14)
    whole = gout_a[...].astype(F32)
    gd_ref[...] = whole[:, 0:share, :].reshape(gd_ref.shape)
    gp_ref[...] = whole[:, share : 2 * share, :].reshape(gp_ref.shape)

    sent(sendbuf, ns - 1, 0)
    sent(back, ns - 1, 1)
    sent(second_part, nc - 1, 2)
    sent(state_full, nc - 1, 3)
    sent(first_rows, nc - 1, 4)
    sent(we_all, nc - 1, 16)
    sent(wp_all, nc - 1, 17)
    sent(state_rows, nc - 1, 18)
    remote(seven, seven, 19, me, my).wait_send()
    sent(mid_full, nc - 1, 7)
    sent(out_rows, ns - 1, 10)
    sent(proj_part, nc - 1, 11)
    sent(grads_a, ns - 1, 12)
    sent(grads_b, ns - 1, 13)
    sent(gout_a, ns - 1, 14)
    sent(gout_b, ns - 1, 15)


def local(
    grid_state,
    cotangent,
    encoder_weight,
    processor_weight,
    decoder_weight,
    g2m_send,
    g2m_edges,
    m2g_send,
    m2g_edges,
    m2m_edges,
):
    ns = lax.axis_size("space")
    nc = lax.axis_size("chan")
    grid_rows, width = grid_state.shape
    mesh, fan = g2m_edges.shape
    fan_m = m2m_edges.shape[1]
    fan_d = m2g_edges.shape[1]
    cap = g2m_send.shape[1]
    cap2 = m2g_send.shape[1]
    reach = min(REACH, mesh // 2)
    full = encoder_weight.shape[0]
    share = full // ns
    pad2 = (cap2 + 15) // 16 * 16
    tall = 8 if ns % 8 == 0 else ns
    send = g2m_send.reshape(ns // tall, tall, cap // 128, 128).transpose(0, 2, 1, 3).reshape(-1)
    halves = grid_rows // CHUNK // 2

    vmem = pl.BlockSpec(memory_space=pltpu.VMEM)
    smem = pl.BlockSpec(memory_space=pltpu.SMEM)
    weight = pltpu.VMEM((full, width), F32)
    return tuple(
        pl.pallas_call(
            functools.partial(kernel, (ns, nc, fan, fan_m, fan_d)),
            out_shape=(
                pltpu.VMEM(grid_state.shape, BF16),
                weight,
                weight,
                weight,
            ),
            in_specs=[pl.BlockSpec(memory_space=pltpu.HBM)] * 5 + [smem] + [vmem] * 4,
            out_specs=(vmem,) * 4,
            scratch_shapes=[
                pltpu.VMEM((grid_rows, width), BF16),
                pltpu.VMEM((grid_rows, width), BF16),
                pltpu.VMEM((nc, full, width), BF16),
                pltpu.VMEM((nc, full, width), BF16),
                pltpu.VMEM((full, width), BF16),
                pltpu.VMEM((grid_rows, width), F32),
                pltpu.VMEM((cap, width), F32),
                pltpu.VMEM((ns, cap, width), BF16),
                pltpu.VMEM((ns, cap, width), BF16),
                pltpu.VMEM((halves, ns * cap2, CHUNK), BF16),
                pltpu.VMEM((halves, ns * cap2, CHUNK), BF16),
                pltpu.VMEM((mesh, fan), F32),
                pltpu.VMEM((mesh // 8, 8 * fan), jnp.int32),
                pltpu.VMEM((mesh // 8, 8 * fan), jnp.int32),
                pltpu.VMEM((ns, mesh, cap), BF16),
                pltpu.VMEM((ns * cap2, width), F32),
                pltpu.VMEM((ns, pad2, width), BF16),
                pltpu.VMEM((ns, pad2, width), BF16),
                pltpu.VMEM((ns * pad2, mesh), F32),
                pltpu.VMEM((ns * pad2, mesh), BF16),
                pltpu.VMEM((mesh, ns * pad2), BF16),
                pltpu.VMEM((mesh, mesh + 2 * reach), BF16),
                pltpu.VMEM((mesh + 2 * reach, mesh), BF16),
                pltpu.VMEM((mesh, width), BF16),
                pltpu.VMEM((nc, mesh, width), BF16),
                pltpu.VMEM((nc, mesh, width), BF16),
                pltpu.VMEM((mesh, width), F32),
                pltpu.VMEM((mesh, width), F32),
                pltpu.VMEM((nc, mesh, width), BF16),
                pltpu.VMEM((nc, mesh // nc, width), BF16),
                pltpu.VMEM((mesh, width), F32),
                pltpu.VMEM((nc, mesh // nc, full), BF16),
                pltpu.VMEM((nc, mesh // nc, width), BF16),
                pltpu.VMEM((mesh + 2 * reach, width), BF16),
                pltpu.VMEM((nc, mesh, width), BF16),
                pltpu.VMEM((ns, pad2, width), BF16),
                pltpu.VMEM((ns, pad2, width), BF16),
                pltpu.VMEM((width, ns * cap2), BF16),
                pltpu.VMEM((mesh + 2 * reach, width), F32),
                pltpu.VMEM((reach, width), F32),
                pltpu.VMEM((reach, width), F32),
                pltpu.VMEM((nc, mesh, width), BF16),
                pltpu.VMEM((nc, mesh, width), BF16),
                pltpu.VMEM((ns, 2 * share, width), BF16),
                pltpu.VMEM((ns, share, width), BF16),
                pltpu.VMEM((ns, 2 * share, width), BF16),
                pltpu.VMEM((ns, share, width), BF16),
                pltpu.VMEM((ns, 2 * share, width), BF16),
                pltpu.VMEM((ns, share, width), BF16),
                pltpu.SemaphoreType.DMA((20,)),
                pltpu.SemaphoreType.DMA((20,)),
                pltpu.SemaphoreType.DMA((ns,)),
                pltpu.SemaphoreType.DMA((5,)),
            ],
            compiler_params=pltpu.CompilerParams(
                collective_id=0,
                has_side_effects=True,
                vmem_limit_bytes=56 * 1024 * 1024,
            ),
            cost_estimate=pl.CostEstimate(
                flops=12_000_000_000, bytes_accessed=10_000_000, transcendentals=0
            ),
            name="encode_process_decode",
        )(
            grid_state,
            cotangent,
            encoder_weight,
            processor_weight,
            decoder_weight,
            send,
            g2m_edges.T,
            m2g_send,
            m2g_edges.T,
            m2m_edges.T,
        )
    )


def solution(mesh):
    placed = (P("space", "chan"),) * 2 + (P(None, "chan"),) * 3 + (P("space", None),) * 5
    return jax.shard_map(
        local,
        mesh=mesh,
        in_specs=placed,
        out_specs=(P("space", "chan"),) + (P(None, "chan"),) * 3,
        check_vma=False,
    )
```

```python
import functools

import jax
import jax.numpy as jnp
from jax import lax
from jax.experimental import pallas as pl
from jax.experimental.pallas import tpu as pltpu
from jax.sharding import PartitionSpec as P

REACH = 160
CHUNK = 1024
MESH = pl.DeviceIdType.MESH
F32 = jnp.float32
BF16 = jnp.bfloat16


def dot(a, b):
    return jnp.dot(a, b, preferred_element_type=F32)


def dot_nt(a, b):
    return lax.dot_general(a, b, (((1,), (1,)), ((), ())), preferred_element_type=F32)


def dot_tn(a, b):
    return lax.dot_general(a, b, (((0,), (0,)), ((), ())), preferred_element_type=F32)


def slope(values):
    sigmoid = jax.nn.sigmoid(values)
    return sigmoid * (1.0 + values * (1.0 - sigmoid))


def row_iota(rows, lanes):
    return lax.broadcasted_iota(jnp.int32, (rows, lanes), 0).astype(F32).astype(BF16)


def ones_where(mask):
    return jnp.where(mask, jnp.ones((), BF16), jnp.zeros((), BF16))


def narrow(row, base):
    return (row - base).astype(F32).astype(BF16)


def kernel(
    sizes,
    grid_hbm,
    cot_hbm,
    we_hbm,
    wp_hbm,
    wd_hbm,
    send_ref,
    source_ref,
    mesh_send_ref,
    edge_ref,
    near_ref,
    pred_ref,
    ge_ref,
    gp_ref,
    gd_ref,
    grid_ref,
    cot_ref,
    we_all,
    wp_all,
    wd_ref,
    grid32,
    stage,
    sendbuf,
    recv,
    at_even,
    at_odd,
    senders,
    key,
    low,
    counts,
    slot_grad,
    back_out,
    back,
    sel32,
    sel,
    selt,
    rim,
    rimt,
    dgrad,
    second_part,
    second_recv,
    second,
    state_sum,
    state_full,
    state_rows,
    gathered,
    first_rows,
    proj_rows,
    ext,
    mid_full,
    out_rows,
    slots,
    slots_t,
    rim_grad,
    halo_low,
    halo_high,
    proj_part,
    proj_recv,
    grads_a,
    grads_b,
    pair_a,
    pair_b,
    half_a,
    half_b,
    grecv_a,
    grecv_b,
    gout_a,
    gout_b,
    ssem,
    rsem,
    gsem,
    isem,
):
    ns, nc, fan, fan_m, fan_d = sizes
    me = lax.axis_index("space")
    my = lax.axis_index("chan")
    grid_rows, width = grid_ref.shape
    cap = recv.shape[1]
    mesh = state_sum.shape[0]
    cap2 = mesh_send_ref.shape[1]
    pad2 = back.shape[1]
    reach = halo_low.shape[0]
    share = grads_b.shape[2]
    full = ge_ref.shape[0]
    fan_scale = fan ** (-0.5)
    fan_m_scale = fan_m ** (-0.5)
    fan_d_scale = fan_d ** (-0.5)
    all_slots = ns * cap2
    nxt = lax.rem(me + 1, ns)
    prv = lax.rem(me + ns - 1, ns)

    def remote(src, dst, which, space, chan, rec=None):
        return pltpu.make_async_remote_copy(
            src_ref=src,
            dst_ref=dst,
            send_sem=ssem.at[which],
            recv_sem=rsem.at[which] if rec is None else rec,
            device_id=(space, chan),
            device_id_type=MESH,
        )

    side = 4 if ns == 32 else 1

    def at_distance(k, sign):
        if side == 1:
            return lax.rem(me + ns + sign * k, ns)
        along_x = lax.rem(me // 8 + side + sign * lax.rem(k, side), side)
        along_y = lax.rem(me // 2 + side + sign * lax.rem(k // side, side), side)
        return along_x * 8 + along_y * 2 + lax.rem(me + k // 16, 2)

    def peers(body, lo=1, hi=ns):
        def step(k, carry):
            body(at_distance(k, 1))
            return carry

        lax.fori_loop(lo, hi, step, 0)

    def chans(body):
        for k in range(1, nc):
            body(lax.rem(my + k, nc))

    def wait_chan(buf, which):
        part = buf.at[pl.ds(0, nc - 1)]
        remote(part, part, which, me, my).wait_recv()

    def wait_space(buf, which):
        part = buf.at[pl.ds(0, ns - 1)]
        remote(part, part, which, me, my).wait_recv()

    def sent(buf, count, which):
        part = buf.at[pl.ds(0, count)]
        remote(part, part, which, me, my).wait_send()

    loads = [
        pltpu.make_async_copy(src, dst, isem.at[i])
        for i, (src, dst) in enumerate(
            (
                (grid_hbm, grid_ref),
                (cot_hbm, cot_ref),
                (we_hbm, we_all.at[my]),
                (wp_hbm, wp_all.at[my]),
                (wd_hbm, wd_ref),
            )
        )
    ]
    loads[0].start()
    barrier = pltpu.get_barrier_semaphore()

    def greet(peer):
        pl.semaphore_signal(barrier, inc=1, device_id=(peer, my), device_id_type=MESH)

    peers(greet)

    def greet_chan(c):
        pl.semaphore_signal(barrier, inc=1, device_id=(me, c), device_id_type=MESH)

    chans(greet_chan)

    def greet_beside(c):
        for space in (nxt, prv):
            pl.semaphore_signal(barrier, inc=1, device_id=(space, c), device_id_type=MESH)

    chans(greet_beside)

    for load in loads[1:]:
        load.start()
    loads[0].wait()

    def widen(i, carry):
        rows = pl.ds(pl.multiple_of(i * CHUNK, CHUNK), CHUNK)
        grid32[rows, :] = grid_ref[rows, :].astype(F32)
        return carry

    lax.fori_loop(0, grid_rows // CHUNK, widen, 0)

    lanes = 8 if ns % 8 == 0 else ns

    def pick(peer):
        first_of = (peer // lanes) * (lanes * cap) + lax.rem(peer, lanes) * 128
        for part in range(cap // 128):

            def some(i, carry):
                base = pl.multiple_of(i * 64, 64)
                at = first_of + part * (lanes * 128) + base
                rows = [grid32[pl.ds(send_ref[at + u], 1), :] for u in range(64)]
                for u in range(64):
                    stage[pl.ds(part * 128 + base + u, 1), :] = rows[u]
                return carry

            lax.fori_loop(0, 2, some, 0)

    def pick_for(peer):
        pick(peer)
        sendbuf[peer] = stage[...].astype(BF16)

    def send_picked(peer):
        remote(sendbuf.at[peer], recv.at[me], 0, peer, my, gsem.at[me]).start()

    def pick_and_send(peer):
        pick_for(peer)
        send_picked(peer)

    early = ns // 2
    peers(pick_for, 1, early)

    mesh_send = mesh_send_ref[...].astype(F32).T
    lane_iota = lax.broadcasted_iota(jnp.int32, (cap2, mesh), 1).astype(F32)
    for p in range(ns):
        hot = jnp.where(lane_iota == mesh_send[:, p : p + 1], 1.0, 0.0)
        sel32[p * pad2 : p * pad2 + cap2, :] = hot
        if pad2 > cap2:
            sel32[p * pad2 + cap2 : (p + 1) * pad2, :] = jnp.zeros((pad2 - cap2, mesh), F32)
    sel[...] = sel32[...].astype(BF16)
    selt[...] = sel32[...].T.astype(BF16)

    pl.semaphore_wait(barrier, ns - 1 + 3 * (nc - 1))
    peers(send_picked, 1, early)
    for load in loads[1:]:
        load.wait()

    def send_weights(c):
        remote(we_all.at[my], we_all.at[my], 16, me, c).start()
        remote(wp_all.at[my], wp_all.at[my], 17, me, c).start()

    chans(send_weights)

    iota = row_iota(128, 128)
    slot_grad[...] = jnp.zeros(slot_grad.shape, F32)

    steps = grid_rows // CHUNK
    half = all_slots // 2

    def build(buf, at, step, lo, hi):
        start = pl.multiple_of(step * CHUNK, CHUNK)
        rows = edge_ref[:, pl.ds(start, CHUNK)]
        for kb in range(lo // 128, hi // 128):
            cut = [narrow(rows[j : j + 1, :], kb * 128) for j in range(fan_d)]
            for lb in range(CHUNK // 128):
                total = None
                for j in range(fan_d):
                    one = ones_where(iota == cut[j][:, lb * 128 : (lb + 1) * 128])
                    total = one if total is None else total + one
                buf[at, kb * 128 : (kb + 1) * 128, lb * 128 : (lb + 1) * 128] = total

    def spread(buf, at, step, lo, hi):
        rows = pl.ds(pl.multiple_of(step * CHUNK, CHUNK), CHUNK)
        slot_grad[lo:hi, :] += dot(buf[at, lo:hi, :], cot_ref[rows, :])

    cuts = [(0, half), (half, all_slots)] if half % 128 == 0 else [(0, all_slots)]
    build(at_even, 0, 0, 0, all_slots)

    def edge_step(t, carry):
        for lo, hi in cuts:
            spread(at_even, t, 2 * t, lo, hi)
            build(at_odd, t, 2 * t + 1, lo, hi)
        for lo, hi in cuts:
            spread(at_odd, t, 2 * t + 1, lo, hi)
            build(at_even, t + 1, 2 * t + 2, lo, hi)
        return carry

    last = steps // 2 - 1
    lax.fori_loop(0, last, edge_step, 0)
    for lo, hi in cuts:
        spread(at_even, last, 2 * last, lo, hi)
        build(at_odd, last, 2 * last + 1, lo, hi)
    spread(at_odd, last, 2 * last + 1, 0, all_slots)
    back_out[:, 0:cap2, :] = (
        (slot_grad[...] * fan_d_scale).reshape(ns, cap2, width).astype(BF16)
    )
    if pad2 > cap2:
        back_out[:, cap2:pad2, :] = jnp.zeros((ns, pad2 - cap2, width), BF16)

    def send_back(peer):
        remote(back_out.at[peer], back.at[me], 1, peer, my).start()

    peers(send_back)
    back[me] = back_out[me]

    peers(pick_and_send, early, ns)
    pick(me)
    recv[me] = stage[...].astype(BF16)

    octets = mesh // 8
    senders[...] = source_ref[...].astype(F32).T
    parts = [
        senders[pl.ds(u, octets, stride=8), :].astype(jnp.int32) for u in range(8)
    ]
    key[...] = jnp.concatenate([(part // cap) * 8 + u for u, part in enumerate(parts)], axis=1)
    low[...] = jnp.concatenate([part % cap for part in parts], axis=1)
    big = row_iota(128, key.shape[1])

    def one_hot(row, rows):
        step = min(rows, 128)
        return jnp.concatenate(
            [ones_where(big[0:step] == narrow(row, base)) for base in range(0, rows, step)], axis=0
        )

    def count_step(g, carry):
        found = []
        for u in range(2):
            row = pl.ds(2 * g + u, 1)
            left = one_hot(key[row, :], 8 * ns)
            found.append(dot_nt(left, one_hot(low[row, :], cap)).reshape(ns, 8, cap))
        rows = pl.ds(pl.multiple_of(g * 16, 16), 16)
        counts[:, rows, :] = jnp.concatenate(found, axis=1).astype(BF16)
        return carry

    lax.fori_loop(0, mesh // 16, count_step, 0, unroll=5 if mesh % 80 == 0 else 1)

    wait_space(back, 1)
    dgrad[...] = dot(selt[...], back[...].reshape(ns * pad2, width)).astype(BF16)
    for c in range(nc):
        second_part[c] = dot_nt(dgrad[...], wd_ref[c * width : (c + 1) * width, :]).astype(BF16)

    def send_second(c):
        remote(second_part.at[c], second_recv.at[my], 2, me, c).start()

    chans(send_second)
    second_recv[my] = second_part[my]
    def absorb(k, waits):
        total = None
        for u in range(4):
            source = at_distance(4 * k + u, -1)
            if waits or u > 0:
                remote(recv.at[source], recv.at[source], 0, me, my, gsem.at[source]).wait_recv()
            term = dot(counts[source], recv[source])
            total = term if total is None else total + term
        return total

    state_sum[...] = absorb(0, False)

    def absorb_step(k, carry):
        state_sum[...] += absorb(k, True)
        return carry

    lax.fori_loop(1, ns // 4, absorb_step, 0)
    state_full[my] = state_sum[...].astype(BF16)

    piece = mesh // nc
    own_piece = pl.ds(pl.multiple_of(my * piece, 16), piece)

    def send_rows_of_sum(c):
        rows = pl.ds(pl.multiple_of(c * piece, 16), piece)
        remote(state_full.at[my, rows], state_rows.at[my], 18, me, c).start()

    chans(send_rows_of_sum)
    state_rows[my] = state_full[my, own_piece, :]

    def send_state(c):
        remote(state_full.at[my], state_full.at[my], 3, me, c).start()

    chans(send_state)

    node = lax.broadcasted_iota(jnp.int32, near_ref.shape, 1)
    span = ns * mesh
    offset = near_ref[...] - me * mesh - node + reach
    offset = jnp.where(offset < 0, offset + span, offset)
    offset = jnp.where(offset >= span, offset - span, offset) + node
    rows_iota = lax.broadcasted_iota(jnp.int32, rimt.shape, 0)
    total = jnp.zeros(rimt.shape, F32)
    for j in range(fan_m):
        total = total + jnp.where(rows_iota == offset[j : j + 1, :], 1.0, 0.0)
    rimt[...] = total.astype(BF16)
    rim[...] = total.T.astype(BF16)
    wait_chan(we_all, 16)
    wait_chan(wp_all, 17)
    wait_chan(state_rows, 18)
    whole = jnp.concatenate([state_rows[c] for c in range(nc)], axis=1)
    total = jnp.concatenate([dot(whole, we_all[c]) for c in range(nc)], axis=1) * fan_scale
    latent = (total * jax.nn.sigmoid(total)).astype(BF16)
    first_rows[my] = latent
    for c in range(nc):
        proj_rows[c] = dot(latent, wp_all[c]).astype(BF16)
    upper = my >= nc // 2
    beside = jnp.where(upper, nxt, prv)
    inner = pl.ds(pl.multiple_of(reach + my * piece, 16), piece)
    outer = pl.ds(
        pl.multiple_of(jnp.where(upper, my * piece - (mesh - reach), reach + mesh + my * piece), 16),
        piece,
    )

    def send_projected(c):
        remote(proj_rows.at[c], ext.at[inner], 19, me, c).start()

    def send_beside(c):
        remote(proj_rows.at[c], ext.at[outer], 19, beside, c).start()

    chans(send_projected)
    send_beside(my)
    chans(send_beside)
    ext[inner, :] = proj_rows[my]

    def send_first(c):
        remote(first_rows.at[my], first_rows.at[my], 4, me, c).start()

    chans(send_first)

    wait_chan(second_recv, 2)
    total = second_recv[0].astype(F32)
    for c in range(1, nc):
        total = total + second_recv[c].astype(F32)
    second[...] = total
    wait_chan(state_full, 3)
    total = dot(state_full[0], we_all[my, 0:width, :])
    for c in range(1, nc):
        total = total + dot(state_full[c], we_all[my, c * width : (c + 1) * width, :])
    gathered[...] = slope(total * fan_scale) * fan_scale
    seven = ext.at[pl.ds(0, (2 * nc - 1) * piece)]
    remote(seven, seven, 19, me, my).wait_recv()
    total = dot(rim[...], ext[...]) * fan_m_scale
    sigmoid = jax.nn.sigmoid(total)
    silu = total * sigmoid
    slant = sigmoid * (1.0 + total * (1.0 - sigmoid))
    pre = (second[...] * slant * fan_m_scale).astype(BF16)
    rim_grad[...] = dot(rimt[...], pre)
    down = remote(rim_grad.at[pl.ds(0, reach)], halo_high, 8, prv, my)
    up = remote(rim_grad.at[pl.ds(reach + mesh, reach)], halo_low, 9, nxt, my)
    down.start()
    up.start()
    wait_chan(first_rows, 4)
    own_lanes = pl.ds(pl.multiple_of(my * width, width), width)
    first = first_rows[:, :, own_lanes].reshape(mesh, width).astype(F32)
    mid_full[my] = (first + silu).astype(BF16)

    def send_mid(c):
        remote(mid_full.at[my], mid_full.at[my], 7, me, c).start()

    chans(send_mid)
    down.wait()
    up.wait()
    rim_grad[reach : 2 * reach, :] += halo_low[...]
    rim_grad[mesh : mesh + reach, :] += halo_high[...]
    projected = rim_grad[reach : reach + mesh, :].astype(BF16)
    for c in range(nc):
        proj_part[c] = dot_nt(projected, wp_all[my, c * width : (c + 1) * width, :]).astype(BF16)

    def send_proj(c):
        remote(proj_part.at[c], proj_recv.at[my], 11, me, c).start()

    chans(send_proj)
    proj_recv[my] = proj_part[my]

    wait_chan(mid_full, 7)
    total = dot(mid_full[0], wd_ref[0:width, :])
    for c in range(1, nc):
        total = total + dot(mid_full[c], wd_ref[c * width : (c + 1) * width, :])
    out_rows[...] = dot(sel[...], total.astype(BF16)).astype(BF16).reshape(out_rows.shape)

    def send_rows(peer):
        remote(out_rows.at[peer], slots.at[me], 10, peer, my).start()

    peers(send_rows)
    slots[me] = out_rows[me]
    core = lax.rem(me, 2)
    pair = me // 2
    sibling = me + 1 - 2 * core
    pairs = ns // 2
    blocks = width // share // 2

    def deal(buf, c, rows, grad):
        parts = grad.reshape(blocks, 2, share, width)
        for u in range(2):
            buf[u, c * blocks : (c + 1) * blocks, rows, :] = parts[:, u]

    def same_core(body):
        def step(k, carry):
            body(lax.rem(me + 2 * k, ns) if side == 1 else at_distance(k, 1))
            return carry

        lax.fori_loop(1, pairs, step, 0)

    def wait_pairs(buf, which):
        part = buf.at[pl.ds(0, pairs - 1)]
        remote(part, part, which, me, my).wait_recv()

    for c in range(nc):
        deal(grads_a, c, slice(0, share), dot_tn(mid_full[c], dgrad[...]))
        latent = first_rows[:, :, c * width : (c + 1) * width].reshape(mesh, width)
        deal(grads_a, c, slice(share, 2 * share), dot_tn(latent, projected))

    swap_a = remote(grads_a.at[1 - core], pair_a, 12, sibling, my)
    swap_a.start()
    wait_chan(proj_recv, 11)
    total = second[...]
    for c in range(nc):
        total = total + proj_recv[c].astype(F32)
    sum_grad = (total * gathered[...]).astype(BF16)
    for c in range(nc):
        deal(grads_b, c, slice(0, share), dot_tn(state_full[c], sum_grad))
    swap_b = remote(grads_b.at[1 - core], pair_b, 13, sibling, my)
    swap_b.start()
    swap_a.wait()
    half_a[...] = (grads_a[core] + pair_a[...]).astype(BF16)
    grecv_a[pair] = half_a[pair]

    def send_a(peer):
        remote(half_a.at[peer // 2], grecv_a.at[pair], 20, peer, my).start()

    def send_b(peer):
        remote(half_b.at[peer // 2], grecv_b.at[pair], 21, peer, my).start()

    swap_b.wait()
    half_b[...] = (grads_b[core] + pair_b[...]).astype(BF16)
    grecv_b[pair] = half_b[pair]
    same_core(send_b)
    same_core(send_a)

    wait_space(slots, 10)
    rows = slots[...].astype(F32)[:, 0:cap2, :].reshape(all_slots, width)
    slots_t[...] = rows.T.astype(BF16)

    def predict(t, carry):
        for u, buf in enumerate((at_even, at_odd)):
            moved = dot(slots_t[...], buf[t]) * fan_d_scale
            rows = pl.ds(pl.multiple_of((2 * t + u) * CHUNK, CHUNK), CHUNK)
            pred_ref[rows, :] = (grid_ref[rows, :].astype(F32) + moved.T).astype(BF16)
        return carry

    def gather_sum(got, whole):
        total = got[0].astype(F32)
        for source in range(1, pairs):
            total = total + got[source].astype(F32)
        whole[core, pair] = total.astype(BF16)

    def send_out_a(peer):
        mine = gout_a.at[core, pair]
        remote(mine, mine, 14, peer, my).start()

    def send_out_b(peer):
        mine = gout_b.at[core, pair]
        remote(mine, mine, 15, peer, my).start()

    cuts = [i * (steps // 2) // 4 for i in range(5)]
    lax.fori_loop(cuts[0], cuts[1], predict, 0)
    wait_pairs(grecv_b, 21)
    gather_sum(grecv_b, gout_b)
    same_core(send_out_b)
    wait_pairs(grecv_a, 20)
    gather_sum(grecv_a, gout_a)
    same_core(send_out_a)
    lax.fori_loop(cuts[1], cuts[2], predict, 0)
    wait_pairs(gout_b.at[core], 15)
    twin_b = remote(gout_b.at[core], gout_b.at[core], 23, sibling, my)
    twin_b.start()
    lax.fori_loop(cuts[2], cuts[3], predict, 0)
    wait_pairs(gout_a.at[core], 14)
    twin_a = remote(gout_a.at[core], gout_a.at[core], 22, sibling, my)
    twin_a.start()
    lax.fori_loop(cuts[3], cuts[4], predict, 0)

    def joined(buf, rows):
        both = jnp.stack([buf[0, :, rows, :], buf[1, :, rows, :]], axis=1)
        return both.astype(F32).reshape(full, width)

    twin_b.wait()
    ge_ref[...] = joined(gout_b, slice(0, share))
    twin_a.wait()
    gd_ref[...] = joined(gout_a, slice(0, share))
    gp_ref[...] = joined(gout_a, slice(share, 2 * share))

    sent(sendbuf, ns - 1, 0)
    sent(back, ns - 1, 1)
    sent(second_part, nc - 1, 2)
    sent(state_full, nc - 1, 3)
    sent(first_rows, nc - 1, 4)
    sent(we_all, nc - 1, 16)
    sent(wp_all, nc - 1, 17)
    sent(state_rows, nc - 1, 18)
    remote(seven, seven, 19, me, my).wait_send()
    sent(mid_full, nc - 1, 7)
    sent(out_rows, ns - 1, 10)
    sent(proj_part, nc - 1, 11)
    sent(half_a, pairs - 1, 20)
    sent(half_b, pairs - 1, 21)
    sent(half_a, pairs - 1, 14)
    sent(half_b, pairs - 1, 15)


def local(
    grid_state,
    cotangent,
    encoder_weight,
    processor_weight,
    decoder_weight,
    g2m_send,
    g2m_edges,
    m2g_send,
    m2g_edges,
    m2m_edges,
):
    ns = lax.axis_size("space")
    nc = lax.axis_size("chan")
    grid_rows, width = grid_state.shape
    mesh, fan = g2m_edges.shape
    fan_m = m2m_edges.shape[1]
    fan_d = m2g_edges.shape[1]
    cap = g2m_send.shape[1]
    cap2 = m2g_send.shape[1]
    reach = min(REACH, mesh // 2)
    full = encoder_weight.shape[0]
    share = full // ns
    pad2 = (cap2 + 15) // 16 * 16
    tall = 8 if ns % 8 == 0 else ns
    send = g2m_send.reshape(ns // tall, tall, cap // 128, 128).transpose(0, 2, 1, 3).reshape(-1)
    halves = grid_rows // CHUNK // 2

    vmem = pl.BlockSpec(memory_space=pltpu.VMEM)
    smem = pl.BlockSpec(memory_space=pltpu.SMEM)
    weight = pltpu.VMEM((full, width), F32)
    return tuple(
        pl.pallas_call(
            functools.partial(kernel, (ns, nc, fan, fan_m, fan_d)),
            out_shape=(
                pltpu.VMEM(grid_state.shape, BF16),
                weight,
                weight,
                weight,
            ),
            in_specs=[pl.BlockSpec(memory_space=pltpu.HBM)] * 5 + [smem] + [vmem] * 4,
            out_specs=(vmem,) * 4,
            scratch_shapes=[
                pltpu.VMEM((grid_rows, width), BF16),
                pltpu.VMEM((grid_rows, width), BF16),
                pltpu.VMEM((nc, full, width), BF16),
                pltpu.VMEM((nc, full, width), BF16),
                pltpu.VMEM((full, width), BF16),
                pltpu.VMEM((grid_rows, width), F32),
                pltpu.VMEM((cap, width), F32),
                pltpu.VMEM((ns, cap, width), BF16),
                pltpu.VMEM((ns, cap, width), BF16),
                pltpu.VMEM((halves, ns * cap2, CHUNK), BF16),
                pltpu.VMEM((halves, ns * cap2, CHUNK), BF16),
                pltpu.VMEM((mesh, fan), F32),
                pltpu.VMEM((mesh // 8, 8 * fan), jnp.int32),
                pltpu.VMEM((mesh // 8, 8 * fan), jnp.int32),
                pltpu.VMEM((ns, mesh, cap), BF16),
                pltpu.VMEM((ns * cap2, width), F32),
                pltpu.VMEM((ns, pad2, width), BF16),
                pltpu.VMEM((ns, pad2, width), BF16),
                pltpu.VMEM((ns * pad2, mesh), F32),
                pltpu.VMEM((ns * pad2, mesh), BF16),
                pltpu.VMEM((mesh, ns * pad2), BF16),
                pltpu.VMEM((mesh, mesh + 2 * reach), BF16),
                pltpu.VMEM((mesh + 2 * reach, mesh), BF16),
                pltpu.VMEM((mesh, width), BF16),
                pltpu.VMEM((nc, mesh, width), BF16),
                pltpu.VMEM((nc, mesh, width), BF16),
                pltpu.VMEM((mesh, width), F32),
                pltpu.VMEM((mesh, width), F32),
                pltpu.VMEM((nc, mesh, width), BF16),
                pltpu.VMEM((nc, mesh // nc, width), BF16),
                pltpu.VMEM((mesh, width), F32),
                pltpu.VMEM((nc, mesh // nc, full), BF16),
                pltpu.VMEM((nc, mesh // nc, width), BF16),
                pltpu.VMEM((mesh + 2 * reach, width), BF16),
                pltpu.VMEM((nc, mesh, width), BF16),
                pltpu.VMEM((ns, pad2, width), BF16),
                pltpu.VMEM((ns, pad2, width), BF16),
                pltpu.VMEM((width, ns * cap2), BF16),
                pltpu.VMEM((mesh + 2 * reach, width), F32),
                pltpu.VMEM((reach, width), F32),
                pltpu.VMEM((reach, width), F32),
                pltpu.VMEM((nc, mesh, width), BF16),
                pltpu.VMEM((nc, mesh, width), BF16),
                pltpu.VMEM((2, ns // 2, 2 * share, width), F32),
                pltpu.VMEM((2, ns // 2, share, width), F32),
                pltpu.VMEM((ns // 2, 2 * share, width), F32),
                pltpu.VMEM((ns // 2, share, width), F32),
                pltpu.VMEM((ns // 2, 2 * share, width), BF16),
                pltpu.VMEM((ns // 2, share, width), BF16),
                pltpu.VMEM((ns // 2, 2 * share, width), BF16),
                pltpu.VMEM((ns // 2, share, width), BF16),
                pltpu.VMEM((2, ns // 2, 2 * share, width), BF16),
                pltpu.VMEM((2, ns // 2, share, width), BF16),
                pltpu.SemaphoreType.DMA((24,)),
                pltpu.SemaphoreType.DMA((24,)),
                pltpu.SemaphoreType.DMA((ns,)),
                pltpu.SemaphoreType.DMA((5,)),
            ],
            compiler_params=pltpu.CompilerParams(
                collective_id=0,
                has_side_effects=True,
                vmem_limit_bytes=56 * 1024 * 1024,
            ),
            cost_estimate=pl.CostEstimate(
                flops=12_000_000_000, bytes_accessed=10_000_000, transcendentals=0
            ),
            name="encode_process_decode",
        )(
            grid_state,
            cotangent,
            encoder_weight,
            processor_weight,
            decoder_weight,
            send,
            g2m_edges.T,
            m2g_send,
            m2g_edges.T,
            m2m_edges.T,
        )
    )


def solution(mesh):
    placed = (P("space", "chan"),) * 2 + (P(None, "chan"),) * 3 + (P("space", None),) * 5
    return jax.shard_map(
        local,
        mesh=mesh,
        in_specs=placed,
        out_specs=(P("space", "chan"),) + (P(None, "chan"),) * 3,
        check_vma=False,
    )
```
